128 devices in a mesh: chan: 16 (over x, z_lo, core), beam: 8 (over z_hi, y).
Axes of the slice: x: 4, y: 4, z: 4 (z_hi: 2, z_lo: 2; z = z_hi * 2 + z_lo), core: 2. Of those that a mesh axis runs over, the one named last changes fastest.
Arguments:
- voltages: bfloat16 [512, 2048, 128], P(('chan', 'beam')), may hold values from -6 to 6
- station_map: int32 [512], replicated, may hold values from 0 to 511, each once
- delay: float32 [512, 512], replicated, may hold values from -2 to 2
- screen: float32 [64, 512], replicated, may hold values from -3 to 3
- beam_patch: int32 [512], replicated, may hold values from 0 to 63
Outputs:
- stokes: bfloat16 [512, 32, 2048], P(('beam', 'chan'))
The draws below stay inside these ranges and needn't reach their ends.
Inputs may be any that keep to these rules, and one draw needn't show every extreme that they name: `station_map`: every station appears in exactly one slot.
All inputs are finite; a program needn't handle non-finite values.
Results may differ from the reference program's by a relative error of at most 0.0045.
Values may be sent and summed in bfloat16 or wider, within the bound.
A program may use at most 64 MiB of HBM per device.

```python
import math
import jax
import jax.numpy as jnp
from jax import lax

STATIONS = 512
CHANNELS = 2048
BEAMS = 512
TSAMP = 32
PATCHES = 64


def plant(drawn, own_key, least, high):
    shape = drawn.shape
    index_at = [jax.random.randint(jax.random.fold_in(own_key, axis), (), 0, shape[axis]) for axis in range(len(shape))]
    drawn = drawn.at[tuple(index_at)].set(least)
    longest = shape.index(max(shape))
    index_at[longest] = (index_at[longest] + 1) % shape[longest]
    return drawn.at[tuple(index_at)].set(high)


def levels(rng, extent, split, least, high):
    def one(position, parts):
        draws = jax.random.uniform(jax.random.fold_in(jax.random.fold_in(rng, 6), position), (parts,), jnp.float32, least / len(split), high / len(split))
        return jnp.repeat(jnp.exp(draws), extent[position] // parts).reshape((-1,) + (1,) * (len(extent) - position - 1))

    level = one(*split[0])
    for cut in split[1:]:
        level = level * one(*cut)
    return level


def scatter_about(own_key, extent, scale, limit, split=(), kind=jnp.bfloat16):
    entries = scale * jax.random.normal(own_key, extent, jnp.float32)
    if split:
        entries = entries * levels(own_key, extent, split, -0.22, 0.18)
    return jnp.clip(entries, -limit, limit).astype(kind)


def setup_inputs(seed: int = 0) -> dict:
    streams_of = jax.random.split(jax.random.key(seed), 6)
    return {
        "voltages": scatter_about(streams_of[0], (STATIONS, CHANNELS, 4 * TSAMP), 1.0, 6.0, ((0, 128),)),
        "station_map": jax.random.permutation(streams_of[1], STATIONS).astype(jnp.int32),
        "delay": jnp.clip(jax.random.uniform(streams_of[2], (BEAMS, STATIONS), jnp.float32, -2.0, 2.0), -2.0, 2.0),
        "screen": jnp.clip(jax.random.uniform(streams_of[3], (PATCHES, STATIONS), jnp.float32, -3.0, 3.0), -3.0, 3.0),
        "beam_patch": plant(jax.random.randint(streams_of[4], (BEAMS,), 0, PATCHES), jax.random.fold_in(streams_of[4], 1), 0, PATCHES - 1).astype(jnp.int32),
    }


low_freq = 50.0
band_width = 300.0
ref_freq = 150.0
two_pi = 2.0 * math.pi

def reference(voltages, station_map, delay, screen, beam_patch):
    stations = voltages.shape[0]
    total = voltages.shape[1]
    width = voltages.shape[2]
    beams = delay.shape[0]
    half = width // 2
    scale = 1.0 / math.sqrt(stations)
    delay_cols = jnp.take(delay, station_map, axis=1)
    screen_cols = jnp.take(jnp.take(screen, station_map, axis=1), beam_patch, axis=0)
    index = jnp.arange(total, dtype=jnp.int32)
    freqs = low_freq + (index.astype(jnp.float32) + 0.5) * (band_width / total)
    volt = jnp.swapaxes(voltages, 0, 1).astype(jnp.float32)
    group = math.gcd(total, 8)

    def one_group(items):
        freq_group, volt_group = items
        phase = (two_pi * freq_group)[:, None, None] * delay_cols[None] + screen_cols[None] * (ref_freq / freq_group)[:, None, None]
        w_real = (jnp.cos(phase) * scale).astype(jnp.bfloat16).astype(jnp.float32)
        w_imag = (jnp.sin(phase) * scale).astype(jnp.bfloat16).astype(jnp.float32)
        p_part = jnp.einsum('gbs,gsk->gbk', w_real, volt_group)
        q_part = jnp.einsum('gbs,gsk->gbk', w_imag, volt_group)
        real = p_part[..., :half] + q_part[..., half:]
        imag = p_part[..., half:] - q_part[..., :half]
        return jnp.concatenate([real, imag], axis=-1)
    result = lax.map(one_group, (freqs.reshape(total // group, group), volt.reshape(total // group, group, stations, width)))
    result = result.reshape(total, beams, 4, width // 4)
    power = 0.25 * lax.optimization_barrier(jnp.sum(result * result, axis=2))
    return jnp.transpose(power, (1, 2, 0)).astype(jnp.bfloat16)
```

```python
import math

import jax
import jax.numpy as jnp
import numpy as np
from jax import lax
from jax.experimental import pallas as pl
from jax.experimental.pallas import tpu as pltpu
from jax.sharding import PartitionSpec as P

F32, BF16 = jnp.float32, jnp.bfloat16
LOGICAL = pl.DeviceIdType.LOGICAL
STEP = 300.0 / 2048
DEVICES = 128
CHANS = 16
LANES = 128
CHUNKS = 4
PER_CHUNK = DEVICES // CHUNKS


def route():
    every = [(x, y, z, c) for z in range(4) for y in range(4) for x in range(4) for c in range(2)]
    mixed = [every[(j * 37) % 128] for j in range(1, 128)] + [every[0]]
    return sorted(mixed, key=lambda o: -sum(min(a, 4 - a) for a in o[:3]))


ROUTE = route()


def position():
    chan, beam = lax.axis_index("chan"), lax.axis_index("beam")
    return chan // 4, beam % 4, (beam // 4) * 2 + (chan // 2) % 2, chan % 2


def places():
    x, y, z, c = position()
    xs = [(x + d) % 4 for d in range(4)]
    ys = [(y + d) % 4 for d in range(4)]
    zs = [(z + d) % 4 for d in range(4)]
    cs = [(c + d) % 2 for d in range(2)]
    index = ([v * 32 for v in xs], ys, [(v % 2) * 16 + (v // 2) * 4 for v in zs], [v * 8 for v in cs])
    owner = ([v * 4 for v in xs], [v * 16 for v in ys], [(v % 2) * 2 + (v // 2) * 64 for v in zs], cs)
    return index, owner


def at(shares, offset):
    return shares[0][offset[0]] + shares[1][offset[1]] + shares[2][offset[2]] + shares[3][offset[3]]


def fit(fn, odd, terms):
    nodes = (np.cos((2 * np.arange(400) + 1) * np.pi / 800) + 1) / 8
    r = np.sqrt(nodes)
    want = fn(2 * np.pi * r) / (r if odd else 1.0)
    cheb = np.polynomial.chebyshev.Chebyshev.fit(nodes, want, terms - 1, domain=[0, 0.25])
    return [float(v) for v in cheb.convert(kind=np.polynomial.Polynomial).coef]


SIN, COS = fit(np.sin, True, 7), fit(np.cos, False, 8)


def poly(coefs, z):
    total = jnp.full_like(z, coefs[-1])
    for value in coefs[-2::-1]:
        total = total * z + value
    return total


def turn(t):
    r = t - jnp.round(t)
    z = r * r
    return poly(COS, z), r * poly(SIN, z)


def split3(v):
    high = v.astype(BF16)
    rest = v - high.astype(F32)
    mid = rest.astype(BF16)
    low = (rest - mid.astype(F32)).astype(BF16)
    return high, mid, low


def pick(parts, hot, dims):
    total = None
    for part in parts:
        args = (hot, part) if dims == "left" else (part, hot)
        contract = (((0,), (0,)), ((), ())) if dims == "left" else (((1,), (0,)), ((), ()))
        term = lax.dot_general(*args, contract, preferred_element_type=F32)
        total = term if total is None else total + term
    return total


def kernel(
    volt, station_map, delay, screen, beam_patch, offsets, out,
    got, delay_in, screen_in, map_in, patch_in, offs_in, delay_at, screen_at, bend, weights, vperm, acc, power,
    sent, back, load_sem, bar_send, volt_recv, own_sem, out_send, out_recv,
):
    index, owner = places()
    me = at(index, (0, 0, 0, 0))
    x, y, z, c = position()

    loads = [
        pltpu.make_async_copy(src, dst, load_sem.at[i])
        for i, (src, dst) in enumerate(
            [(station_map, map_in), (offsets, offs_in), (delay, delay_in), (screen, screen_in), (beam_patch, patch_in)]
        )
    ]
    for load in loads:
        load.start()
    barrier = pltpu.get_barrier_semaphore()
    for offset in ROUTE[:-1]:
        pl.semaphore_signal(barrier, inc=1, device_id=at(index, offset), device_id_type=LOGICAL)
    own = pltpu.make_async_copy(volt.at[:, pl.ds(me * CHANS, CHANS), :], got.at[DEVICES - 1], own_sem)
    own.start()
    for load in loads:
        load.wait()

    col = lax.broadcasted_iota(jnp.int32, (1, 512), 1)
    sx = jnp.bitwise_and(x - offs_in[0:1, :], 3)
    sy = jnp.bitwise_and(y - offs_in[1:2, :], 3)
    sz = jnp.bitwise_and(z - offs_in[2:3, :], 3)
    sc = jnp.bitwise_and(c - offs_in[3:4, :], 1)
    slot = (sx * 32 + sy + jnp.bitwise_and(sz, 1) * 16 + jnp.right_shift(sz, 1) * 4 + sc * 8) * 4
    slot = slot + jnp.bitwise_and(col, 3)
    rows = lax.broadcasted_iota(jnp.int32, (512, 512), 0)
    order = (rows == slot).astype(F32).astype(BF16)
    names = map_in[...].reshape(1, 512)
    tops = jnp.right_shift(names, 4).astype(F32).astype(BF16)
    lows = jnp.bitwise_and(names, 15).astype(F32).astype(BF16)
    halves = jnp.dot(
        jnp.concatenate([jnp.broadcast_to(tops, (16, 512)), jnp.broadcast_to(lows, (16, 512))], axis=0),
        order,
        preferred_element_type=F32,
    )
    station = (halves[0:1] * 16.0 + halves[16:17]).astype(jnp.int32)
    hot = (rows == station).astype(F32).astype(BF16)
    ordered = pick(split3(delay_in[...]), hot, "right")
    for chunk in range(CHUNKS):
        delay_at[chunk] = ordered[:, chunk * LANES : (chunk + 1) * LANES]
    patches = (
        lax.broadcasted_iota(jnp.int32, (64, 512), 0) == patch_in[...].reshape(1, 512)
    ).astype(F32).astype(BF16)
    ordered = pick(split3(pick(split3(screen_in[...]), hot, "right")), patches, "left")
    for chunk in range(CHUNKS):
        screen_at[chunk] = ordered[:, chunk * LANES : (chunk + 1) * LANES]

    pl.semaphore_wait(barrier, DEVICES - 1)

    sends = []
    for k, offset in enumerate(ROUTE[:-1]):
        to = at(index, offset)
        copy = pltpu.make_async_remote_copy(
            src_ref=volt.at[:, pl.ds(to * CHANS, CHANS), :],
            dst_ref=got.at[k],
            send_sem=bar_send,
            recv_sem=volt_recv.at[k // PER_CHUNK],
            device_id=to,
            device_id_type=LOGICAL,
        )
        copy.start()

    first = (lax.broadcasted_iota(jnp.int32, (8, LANES), 0) * 0 + me * CHANS).astype(F32)

    def freq(k):
        return 50.0 + (first + (k + 0.5)) * STEP

    for k in range(CHANS - 2):
        bend[k] = (2.0 * 150.0 * STEP * STEP) / (freq(k) * freq(k + 1) * freq(k + 2))
    tau = 2.0 * math.pi
    scale = 1.0 / math.sqrt(512.0)
    high = 32

    def fill(i, _):
        chunk = i // 16
        block = i % 16
        j = block // 4
        start = j + 4 * high * (block % 4)
        d = delay_at[chunk, pl.ds(start, high, stride=4), :]
        s = screen_at[chunk, pl.ds(start, high, stride=4), :]
        f0, f1 = freq(0)[0:1], freq(1)[0:1]
        c0, s0 = turn(f0 * d + s * ((150.0 / tau) / f0))
        rc, rs = turn(STEP * d - s * ((150.0 / tau) * STEP / (f0 * f1)))
        wr, wi = c0 * scale, s0 * scale
        here = pl.ds(pl.multiple_of(block * high, high), high)
        for k in range(CHANS):
            weights[k, chunk, here, 0:LANES] = wr.astype(BF16)
            weights[k, chunk, here, LANES : 2 * LANES] = wi.astype(BF16)
            if k < CHANS - 1:
                wr, wi = wr * rc - wi * rs, wr * rs + wi * rc
            if k < CHANS - 2:
                turned = s * bend[k, 0:1, :]
                rc, rs = rc - turned * rs, rs + turned * rc
        return 0

    lax.fori_loop(0, 16 * CHUNKS, fill, 0)

    r = lax.broadcasted_iota(jnp.int32, (256, 256), 0)
    q = lax.broadcasted_iota(jnp.int32, (256, 256), 1)
    swap = (r == jnp.bitwise_and(q, 15) * 16 + jnp.right_shift(q, 4)).astype(F32).astype(BF16)
    lane = lax.broadcasted_iota(jnp.int32, (1, LANES), 1)
    low_half = lane < 64
    even = jnp.bitwise_and(lane, 32) == 0

    for chunk in range(CHUNKS):
        n = PER_CHUNK - (1 if chunk == CHUNKS - 1 else 0)
        landed = got.at[pl.ds(chunk * PER_CHUNK, n)]
        pltpu.make_async_copy(landed, landed, volt_recv.at[chunk]).wait()
        if chunk == CHUNKS - 1:
            own.wait()
        for m in range(PER_CHUNK // 4):
            block = got[pl.ds(chunk * PER_CHUNK + 4 * m, 4)].reshape(256, LANES)
            turned = jnp.dot(swap, block, preferred_element_type=F32)
            other = pltpu.roll(turned, 64, 1)
            other = jnp.where(low_half, other, -other)
            vperm[:, 16 * m : 16 * m + 16, :] = turned.astype(BF16).reshape(CHANS, 16, LANES)
            vperm[:, LANES + 16 * m : LANES + 16 * m + 16, :] = other.astype(BF16).reshape(CHANS, 16, LANES)

        def beams(k, _):
            part = jnp.dot(weights[k, chunk], vperm[k], preferred_element_type=F32)
            if chunk == 0:
                acc[k] = part
            elif chunk < CHUNKS - 1:
                acc[k] += part
            else:
                total = acc[k] + part
                sq = (total * total).reshape(4, LANES, LANES)
                one = jnp.where(low_half, sq[0], sq[2]) + pltpu.roll(jnp.where(low_half, sq[2], sq[0]), 64, 1)
                two = jnp.where(low_half, sq[1], sq[3]) + pltpu.roll(jnp.where(low_half, sq[3], sq[1]), 64, 1)
                both = jnp.where(even, one, two) + jnp.where(even, pltpu.roll(one, 96, 1), pltpu.roll(two, 32, 1))
                power[k] = (0.25 * both).astype(BF16)
            return 0

        lax.fori_loop(0, CHANS, beams, 0)

    for m in range(8):
        block = power[:, 16 * m : 16 * m + 16, :].reshape(256, LANES)
        sent[16 * m : 16 * m + 16] = (
            jnp.dot(swap, block, preferred_element_type=F32).astype(BF16).reshape(16, CHANS, LANES)
        )
    for offset in ROUTE[:-1]:
        pltpu.make_async_remote_copy(
            src_ref=sent.at[at(owner, offset)],
            dst_ref=back.at[me],
            send_sem=out_send,
            recv_sem=out_recv,
            device_id=at(index, offset),
            device_id_type=LOGICAL,
        ).start()
    mine = pltpu.make_async_copy(sent.at[at(owner, (0, 0, 0, 0))], back.at[me], own_sem)
    mine.start()
    mine.wait()
    rest = back.at[pl.ds(0, DEVICES - 1)]
    pltpu.make_async_copy(rest, rest, out_recv).wait()
    eye = (
        lax.broadcasted_iota(jnp.int32, (LANES, LANES), 0) == lax.broadcasted_iota(jnp.int32, (LANES, LANES), 1)
    ).astype(F32).astype(BF16)
    final = lax.dot_general(
        eye, back[...].reshape(DEVICES * CHANS, LANES), (((1,), (1,)), ((), ())), preferred_element_type=F32
    )
    out[...] = final.astype(BF16).reshape(4, 32, DEVICES * CHANS)
    gone = got.at[pl.ds(0, DEVICES - 1)]
    pltpu.make_async_copy(gone, gone, bar_send).wait()
    pltpu.make_async_copy(rest, rest, out_send).wait()


def body(voltages, station_map, delay, screen, beam_patch):
    table = np.zeros((8, 512), np.int32)
    for k, offset in enumerate(ROUTE):
        table[:4, 4 * k : 4 * k + 4] = np.array(offset, np.int32)[:, None]
    anywhere = pl.BlockSpec(memory_space=pl.ANY)
    return pl.pallas_call(
        kernel,
        out_shape=jax.ShapeDtypeStruct((4, 32, DEVICES * CHANS), BF16),
        in_specs=[anywhere] * 6,
        out_specs=pl.BlockSpec(memory_space=pltpu.VMEM),
        scratch_shapes=[
            pltpu.VMEM((DEVICES, 4, CHANS, LANES), BF16),
            pltpu.VMEM((512, 512), F32),
            pltpu.VMEM((64, 512), F32),
            pltpu.VMEM((512,), jnp.int32),
            pltpu.VMEM((512,), jnp.int32),
            pltpu.VMEM((8, 512), jnp.int32),
            pltpu.VMEM((CHUNKS, 512, LANES), F32),
            pltpu.VMEM((CHUNKS, 512, LANES), F32),
            pltpu.VMEM((CHANS, 8, LANES), F32),
            pltpu.VMEM((CHANS, CHUNKS, 512, 2 * LANES), BF16),
            pltpu.VMEM((CHANS, 2 * LANES, LANES), BF16),
            pltpu.VMEM((CHANS, 512, LANES), F32),
            pltpu.VMEM((CHANS, LANES, LANES), BF16),
            pltpu.VMEM((DEVICES, CHANS, LANES), BF16),
            pltpu.VMEM((DEVICES, CHANS, LANES), BF16),
            pltpu.SemaphoreType.DMA((5,)),
            pltpu.SemaphoreType.DMA,
            pltpu.SemaphoreType.DMA((CHUNKS,)),
            pltpu.SemaphoreType.DMA,
            pltpu.SemaphoreType.DMA,
            pltpu.SemaphoreType.DMA,
        ],
        compiler_params=pltpu.CompilerParams(collective_id=0, has_side_effects=True, vmem_limit_bytes=56 * 2**20),
        name="beamform",
    )(voltages, station_map, delay, screen, beam_patch, jnp.asarray(table))


def solution(mesh):
    placed = (P(("chan", "beam"), None, None), P(), P(), P(), P())
    return jax.shard_map(
        body, mesh=mesh, in_specs=placed, out_specs=P(("beam", "chan"), None, None), check_vma=False
    )
```

```python
import math

import jax
import jax.numpy as jnp
import numpy as np
from jax import lax
from jax.experimental import pallas as pl
from jax.experimental.pallas import tpu as pltpu
from jax.sharding import PartitionSpec as P

F32, BF16 = jnp.float32, jnp.bfloat16
LOGICAL = pl.DeviceIdType.LOGICAL
STEP = 300.0 / 2048
DEVICES = 128
CHANS = 16
LANES = 128
CHUNKS = 4
PER_CHUNK = DEVICES // CHUNKS
GROUPS = 2
UNROLL = 4
PART = CHANS // GROUPS
WIDE = 256 // PART


def route():
    every = [(x, y, z, c) for z in range(4) for y in range(4) for x in range(4) for c in range(2)]
    mixed = [every[(j * 37) % 128] for j in range(1, 128)] + [every[0]]
    return sorted(mixed, key=lambda o: -sum(min(a, 4 - a) for a in o[:3]))


ROUTE = route()


def position():
    chan, beam = lax.axis_index("chan"), lax.axis_index("beam")
    return chan // 4, beam % 4, (beam // 4) * 2 + (chan // 2) % 2, chan % 2


def places():
    x, y, z, c = position()
    xs = [(x + d) % 4 for d in range(4)]
    ys = [(y + d) % 4 for d in range(4)]
    zs = [(z + d) % 4 for d in range(4)]
    cs = [(c + d) % 2 for d in range(2)]
    index = ([v * 32 for v in xs], ys, [(v % 2) * 16 + (v // 2) * 4 for v in zs], [v * 8 for v in cs])
    owner = ([v * 4 for v in xs], [v * 16 for v in ys], [(v % 2) * 2 + (v // 2) * 64 for v in zs], cs)
    return index, owner


def at(shares, offset):
    return shares[0][offset[0]] + shares[1][offset[1]] + shares[2][offset[2]] + shares[3][offset[3]]


def fit(fn, odd, terms):
    nodes = (np.cos((2 * np.arange(400) + 1) * np.pi / 800) + 1) / 8
    r = np.sqrt(nodes)
    want = fn(2 * np.pi * r) / (r if odd else 1.0)
    cheb = np.polynomial.chebyshev.Chebyshev.fit(nodes, want, terms - 1, domain=[0, 0.25])
    return [float(v) for v in cheb.convert(kind=np.polynomial.Polynomial).coef]


SIN, COS = fit(np.sin, True, 7), fit(np.cos, False, 8)


def poly(coefs, z):
    total = jnp.full_like(z, coefs[-1])
    for value in coefs[-2::-1]:
        total = total * z + value
    return total


def turn(t):
    r = t - jnp.round(t)
    z = r * r
    return poly(COS, z), r * poly(SIN, z)


def split3(v):
    high = v.astype(BF16)
    rest = v - high.astype(F32)
    mid = rest.astype(BF16)
    low = (rest - mid.astype(F32)).astype(BF16)
    return high, mid, low


def pick(parts, hot, dims):
    total = None
    for part in parts:
        args = (hot, part) if dims == "left" else (part, hot)
        contract = (((0,), (0,)), ((), ())) if dims == "left" else (((1,), (0,)), ((), ()))
        term = lax.dot_general(*args, contract, preferred_element_type=F32)
        total = term if total is None else total + term
    return total


def kernel(
    volt, station_map, delay, screen, beam_patch, offsets, out,
    got, mine_in, delay_in, screen_in, map_in, patch_in, offs_in, delay_at, screen_at, bend, weights, vperm, acc, power,
    sent, back, load_sem, volt_send, volt_recv, own_sem, out_send, out_recv,
):
    index, owner = places()
    me = at(index, (0, 0, 0, 0))
    x, y, z, c = position()

    loads = [
        pltpu.make_async_copy(src, dst, load_sem.at[i])
        for i, (src, dst) in enumerate(
            [(station_map, map_in), (offsets, offs_in), (delay, delay_in), (screen, screen_in), (beam_patch, patch_in)]
        )
    ]
    for load in loads:
        load.start()
    barrier = pltpu.get_barrier_semaphore()
    for offset in ROUTE[:-1]:
        pl.semaphore_signal(barrier, inc=1, device_id=at(index, offset), device_id_type=LOGICAL)
    own = pltpu.make_async_copy(volt.at[:, pl.ds(me * GROUPS, GROUPS), :, :], mine_in, own_sem)
    own.start()
    pl.semaphore_wait(barrier, DEVICES - 1)

    def send(group):
        for k, offset in enumerate(ROUTE[:-1]):
            to = at(index, offset)
            pltpu.make_async_remote_copy(
                src_ref=volt.at[:, to * GROUPS + group, :, :],
                dst_ref=got.at[group, k],
                send_sem=volt_send.at[group],
                recv_sem=volt_recv.at[group, k // PER_CHUNK],
                device_id=to,
                device_id_type=LOGICAL,
            ).start()

    send(0)
    for load in loads:
        load.wait()

    col = lax.broadcasted_iota(jnp.int32, (1, 512), 1)
    sx = jnp.bitwise_and(x - offs_in[0:1, :], 3)
    sy = jnp.bitwise_and(y - offs_in[1:2, :], 3)
    sz = jnp.bitwise_and(z - offs_in[2:3, :], 3)
    sc = jnp.bitwise_and(c - offs_in[3:4, :], 1)
    slot = (sx * 32 + sy + jnp.bitwise_and(sz, 1) * 16 + jnp.right_shift(sz, 1) * 4 + sc * 8) * 4
    slot = slot + jnp.bitwise_and(col, 3)
    rows = lax.broadcasted_iota(jnp.int32, (512, 512), 0)
    order = (rows == slot).astype(F32).astype(BF16)
    names = map_in[...].reshape(1, 512)
    tops = jnp.right_shift(names, 4).astype(F32).astype(BF16)
    lows = jnp.bitwise_and(names, 15).astype(F32).astype(BF16)
    halves = jnp.dot(
        jnp.concatenate([jnp.broadcast_to(tops, (16, 512)), jnp.broadcast_to(lows, (16, 512))], axis=0),
        order,
        preferred_element_type=F32,
    )
    station = (halves[0:1] * 16.0 + halves[16:17]).astype(jnp.int32)
    hot = (rows == station).astype(F32).astype(BF16)
    ordered = pick(split3(delay_in[...]), hot, "right")
    for chunk in range(CHUNKS):
        delay_at[chunk] = ordered[:, chunk * LANES : (chunk + 1) * LANES]
    patches = (
        lax.broadcasted_iota(jnp.int32, (64, 512), 0) == patch_in[...].reshape(1, 512)
    ).astype(F32).astype(BF16)
    ordered = pick(split3(pick(split3(screen_in[...]), hot, "right")), patches, "left")
    for chunk in range(CHUNKS):
        screen_at[chunk] = ordered[:, chunk * LANES : (chunk + 1) * LANES]

    send(1)

    first = (lax.broadcasted_iota(jnp.int32, (8, LANES), 0) * 0 + me * CHANS).astype(F32)

    def freq(k):
        return 50.0 + (first + (k + 0.5)) * STEP

    for k in range(CHANS - 2):
        bend[k] = (2.0 * 150.0 * STEP * STEP) / (freq(k) * freq(k + 1) * freq(k + 2))
    tau = 2.0 * math.pi
    scale = 1.0 / math.sqrt(512.0)
    high = 32

    def fill(i, _):
        chunk = i // 16
        block = i % 16
        j = block // 4
        start = j + 4 * high * (block % 4)
        d = delay_at[chunk, pl.ds(start, high, stride=4), :]
        s = screen_at[chunk, pl.ds(start, high, stride=4), :]
        f0, f1 = freq(0)[0:1], freq(1)[0:1]
        c0, s0 = turn(f0 * d + s * ((150.0 / tau) / f0))
        rc, rs = turn(STEP * d - s * ((150.0 / tau) * STEP / (f0 * f1)))
        wr, wi = c0 * scale, s0 * scale
        here = pl.ds(pl.multiple_of(block * high, high), high)
        for k in range(CHANS):
            weights[k, chunk, here, 0:LANES] = wr.astype(BF16)
            weights[k, chunk, here, LANES : 2 * LANES] = wi.astype(BF16)
            if k < CHANS - 1:
                wr, wi = wr * rc - wi * rs, wr * rs + wi * rc
            if k < CHANS - 2:
                turned = s * bend[k, 0:1, :]
                rc, rs = rc - turned * rs, rs + turned * rc
        return 0

    lax.fori_loop(0, 16 * CHUNKS, fill, 0)

    r = lax.broadcasted_iota(jnp.int32, (256, 256), 0)
    q = lax.broadcasted_iota(jnp.int32, (256, 256), 1)
    apart = (r == (q % PART) * WIDE + q // PART).astype(F32).astype(BF16)
    together = (q == (r % PART) * WIDE + r // PART).astype(F32).astype(BF16)
    lane = lax.broadcasted_iota(jnp.int32, (1, LANES), 1)
    low_half = lane < 64
    even = jnp.bitwise_and(lane, 32) == 0
    own.wait()

    for group in range(GROUPS):
        got[group, DEVICES - 1] = mine_in[:, group]
        for chunk in range(CHUNKS):
            n = PER_CHUNK - (1 if chunk == CHUNKS - 1 else 0)
            landed = got.at[group, pl.ds(chunk * PER_CHUNK, n)]
            pltpu.make_async_copy(landed, landed, volt_recv.at[group, chunk]).wait()
            srcs = WIDE // 4
            for m in range(PER_CHUNK // srcs):
                block = got[group, pl.ds(chunk * PER_CHUNK + srcs * m, srcs)].reshape(256, LANES)
                turned = jnp.dot(apart, block, preferred_element_type=F32)
                other = pltpu.roll(turned, 64, 1)
                other = jnp.where(low_half, other, -other)
                here = WIDE * m
                vperm[:, here : here + WIDE, :] = turned.astype(BF16).reshape(PART, WIDE, LANES)
                vperm[:, LANES + here : LANES + here + WIDE, :] = other.astype(BF16).reshape(PART, WIDE, LANES)

            def beams(step, _):
                for u in range(UNROLL):
                    k = step * UNROLL + u
                    part = jnp.dot(weights[group * PART + k, chunk], vperm[k], preferred_element_type=F32)
                    if chunk == 0:
                        acc[k] = part
                    elif chunk < CHUNKS - 1:
                        acc[k] += part
                    else:
                        total = acc[k] + part
                        sq = (total * total).reshape(4, LANES, LANES)
                        one = jnp.where(low_half, sq[0], sq[2])
                        one += pltpu.roll(jnp.where(low_half, sq[2], sq[0]), 64, 1)
                        two = jnp.where(low_half, sq[1], sq[3])
                        two += pltpu.roll(jnp.where(low_half, sq[3], sq[1]), 64, 1)
                        both = jnp.where(even, one, two)
                        both += jnp.where(even, pltpu.roll(one, 96, 1), pltpu.roll(two, 32, 1))
                        power[k] = (0.25 * both).astype(BF16)
                return 0

            lax.fori_loop(0, PART // UNROLL, beams, 0)

        for m in range(DEVICES // WIDE):
            block = power[:, WIDE * m : WIDE * m + WIDE, :].reshape(256, LANES)
            sent[group, WIDE * m : WIDE * m + WIDE] = (
                jnp.dot(together, block, preferred_element_type=F32).astype(BF16).reshape(WIDE, PART, LANES)
            )
        for offset in ROUTE[:-1]:
            pltpu.make_async_remote_copy(
                src_ref=sent.at[group, at(owner, offset)],
                dst_ref=back.at[me, group],
                send_sem=out_send.at[group],
                recv_sem=out_recv,
                device_id=at(index, offset),
                device_id_type=LOGICAL,
            ).start()
        back[me, group] = sent[group, at(owner, (0, 0, 0, 0))]

    rest = back.at[pl.ds(0, DEVICES - 1)]
    pltpu.make_async_copy(rest, rest, out_recv).wait()
    eye = (
        lax.broadcasted_iota(jnp.int32, (LANES, LANES), 0) == lax.broadcasted_iota(jnp.int32, (LANES, LANES), 1)
    ).astype(F32).astype(BF16)
    final = lax.dot_general(
        eye, back[...].reshape(DEVICES * CHANS, LANES), (((1,), (1,)), ((), ())), preferred_element_type=F32
    )
    out[...] = final.astype(BF16).reshape(4, 32, DEVICES * CHANS)
    for group in range(GROUPS):
        gone = got.at[group, pl.ds(0, DEVICES - 1)]
        pltpu.make_async_copy(gone, gone, volt_send.at[group]).wait()
        gone = sent.at[group, pl.ds(0, DEVICES - 1)]
        pltpu.make_async_copy(gone, gone, out_send.at[group]).wait()


def body(voltages, station_map, delay, screen, beam_patch):
    table = np.zeros((8, 512), np.int32)
    for k, offset in enumerate(ROUTE):
        table[:4, 4 * k : 4 * k + 4] = np.array(offset, np.int32)[:, None]
    anywhere = pl.BlockSpec(memory_space=pl.ANY)
    return pl.pallas_call(
        kernel,
        out_shape=jax.ShapeDtypeStruct((4, 32, DEVICES * CHANS), BF16),
        in_specs=[anywhere] * 6,
        out_specs=pl.BlockSpec(memory_space=pltpu.VMEM),
        scratch_shapes=[
            pltpu.VMEM((GROUPS, DEVICES, 4, PART, LANES), BF16),
            pltpu.VMEM((4, GROUPS, PART, LANES), BF16),
            pltpu.VMEM((512, 512), F32),
            pltpu.VMEM((64, 512), F32),
            pltpu.VMEM((512,), jnp.int32),
            pltpu.VMEM((512,), jnp.int32),
            pltpu.VMEM((8, 512), jnp.int32),
            pltpu.VMEM((CHUNKS, 512, LANES), F32),
            pltpu.VMEM((CHUNKS, 512, LANES), F32),
            pltpu.VMEM((CHANS, 8, LANES), F32),
            pltpu.VMEM((CHANS, CHUNKS, 512, 2 * LANES), BF16),
            pltpu.VMEM((PART, 2 * LANES, LANES), BF16),
            pltpu.VMEM((PART, 512, LANES), F32),
            pltpu.VMEM((PART, LANES, LANES), BF16),
            pltpu.VMEM((GROUPS, DEVICES, PART, LANES), BF16),
            pltpu.VMEM((DEVICES, GROUPS, PART, LANES), BF16),
            pltpu.SemaphoreType.DMA((5,)),
            pltpu.SemaphoreType.DMA((GROUPS,)),
            pltpu.SemaphoreType.DMA((GROUPS, CHUNKS)),
            pltpu.SemaphoreType.DMA,
            pltpu.SemaphoreType.DMA((GROUPS,)),
            pltpu.SemaphoreType.DMA,
        ],
        compiler_params=pltpu.CompilerParams(collective_id=0, has_side_effects=True, vmem_limit_bytes=56 * 2**20),
        name="beamform",
    )(voltages.reshape(4, DEVICES * GROUPS, PART, LANES), station_map, delay, screen, beam_patch, jnp.asarray(table))


def solution(mesh):
    placed = (P(("chan", "beam"), None, None), P(), P(), P(), P())
    return jax.shard_map(
        body, mesh=mesh, in_specs=placed, out_specs=P(("beam", "chan"), None, None), check_vma=False
    )
```

```python
import math

import jax
import jax.numpy as jnp
import numpy as np
from jax import lax
from jax.experimental import pallas as pl
from jax.experimental.pallas import tpu as pltpu
from jax.sharding import PartitionSpec as P

F32, BF16 = jnp.float32, jnp.bfloat16
LOGICAL = pl.DeviceIdType.LOGICAL
STEP = 300.0 / 2048
DEVICES = 128
CHANS = 16
LANES = 128
CHUNKS = 4
PER_CHUNK = DEVICES // CHUNKS
GROUPS = 2
UNROLL = 8
PART = CHANS // GROUPS
WIDE = 256 // PART


def hops(offset):
    return sum(min(a, 4 - a) for a in offset[:3])


def route():
    order = []
    for total in (2, 3, 1, 0):
        quarter = []
        for a in range(4):
            for b in range(4):
                dx, dy = b, (a + b) % 4
                quarter += [(dx, dy, (total - dx - dy) % 4, core) for core in (1, 0)]
        order += sorted(quarter, key=lambda o: -hops(o))
    own = (0, 0, 0, 0)
    return [o for o in order if o != own] + [own]


ROUTE = route()
OUT_ROUTE = sorted(ROUTE, key=lambda o: -hops(o))


def position():
    chan, beam = lax.axis_index("chan"), lax.axis_index("beam")
    return chan // 4, beam % 4, (beam // 4) * 2 + (chan // 2) % 2, chan % 2


def places():
    x, y, z, c = position()
    xs = [(x + d) % 4 for d in range(4)]
    ys = [(y + d) % 4 for d in range(4)]
    zs = [(z + d) % 4 for d in range(4)]
    cs = [(c + d) % 2 for d in range(2)]
    index = ([v * 32 for v in xs], ys, [(v % 2) * 16 + (v // 2) * 4 for v in zs], [v * 8 for v in cs])
    owner = ([v * 4 for v in xs], [v * 16 for v in ys], [(v % 2) * 2 + (v // 2) * 64 for v in zs], cs)
    return index, owner


def at(shares, offset):
    return shares[0][offset[0]] + shares[1][offset[1]] + shares[2][offset[2]] + shares[3][offset[3]]


def fit(fn, odd, terms):
    nodes = (np.cos((2 * np.arange(400) + 1) * np.pi / 800) + 1) / 8
    r = np.sqrt(nodes)
    want = fn(2 * np.pi * r) / (r if odd else 1.0)
    cheb = np.polynomial.chebyshev.Chebyshev.fit(nodes, want, terms - 1, domain=[0, 0.25])
    return [float(v) for v in cheb.convert(kind=np.polynomial.Polynomial).coef]


SIN, COS = fit(np.sin, True, 7), fit(np.cos, False, 8)


def poly(coefs, z):
    total = jnp.full_like(z, coefs[-1])
    for value in coefs[-2::-1]:
        total = total * z + value
    return total


def turn(t):
    r = t - jnp.round(t)
    z = r * r
    return poly(COS, z), r * poly(SIN, z)


def split3(v):
    high = v.astype(BF16)
    rest = v - high.astype(F32)
    mid = rest.astype(BF16)
    low = (rest - mid.astype(F32)).astype(BF16)
    return high, mid, low


def pick(parts, hot, dims):
    total = None
    for part in parts:
        args = (hot, part) if dims == "left" else (part, hot)
        contract = (((0,), (0,)), ((), ())) if dims == "left" else (((1,), (0,)), ((), ()))
        term = lax.dot_general(*args, contract, preferred_element_type=F32)
        total = term if total is None else total + term
    return total


def kernel(
    volt, station_map, delay, screen, beam_patch, offsets, out,
    got, mine_in, delay_in, screen_in, map_in, patch_in, offs_in, delay_at, screen_at, bend, weights, vperm, acc, power,
    sent, back, load_sem, volt_send, volt_recv, own_sem, out_send, out_recv,
):
    index, owner = places()
    me = at(index, (0, 0, 0, 0))
    x, y, z, c = position()

    loads = [
        pltpu.make_async_copy(src, dst, load_sem.at[i])
        for i, (src, dst) in enumerate(
            [(station_map, map_in), (offsets, offs_in), (delay, delay_in), (screen, screen_in), (beam_patch, patch_in)]
        )
    ]
    for load in loads:
        load.start()
    barrier = pltpu.get_barrier_semaphore()
    for offset in OUT_ROUTE[:-1]:
        pl.semaphore_signal(barrier, inc=1, device_id=at(index, offset), device_id_type=LOGICAL)
    own = pltpu.make_async_copy(volt.at[:, pl.ds(me * GROUPS, GROUPS), :, :], mine_in, own_sem)
    own.start()
    pl.semaphore_wait(barrier, DEVICES - 1)

    def send(group):
        for k, offset in enumerate(ROUTE[:-1]):
            to = at(index, offset)
            pltpu.make_async_remote_copy(
                src_ref=volt.at[:, to * GROUPS + group, :, :],
                dst_ref=got.at[group, k],
                send_sem=volt_send.at[group],
                recv_sem=volt_recv.at[group, k // PER_CHUNK],
                device_id=to,
                device_id_type=LOGICAL,
            ).start()

    send(0)
    for load in loads:
        load.wait()

    col = lax.broadcasted_iota(jnp.int32, (1, 512), 1)
    sx = jnp.bitwise_and(x - offs_in[0:1, :], 3)
    sy = jnp.bitwise_and(y - offs_in[1:2, :], 3)
    sz = jnp.bitwise_and(z - offs_in[2:3, :], 3)
    sc = jnp.bitwise_and(c - offs_in[3:4, :], 1)
    slot = (sx * 32 + sy + jnp.bitwise_and(sz, 1) * 16 + jnp.right_shift(sz, 1) * 4 + sc * 8) * 4
    slot = slot + jnp.bitwise_and(col, 3)
    rows = lax.broadcasted_iota(jnp.int32, (512, 512), 0)
    order = (rows == slot).astype(F32).astype(BF16)
    names = map_in[...].reshape(1, 512)
    tops = jnp.right_shift(names, 4).astype(F32).astype(BF16)
    lows = jnp.bitwise_and(names, 15).astype(F32).astype(BF16)
    halves = jnp.dot(
        jnp.concatenate([jnp.broadcast_to(tops, (16, 512)), jnp.broadcast_to(lows, (16, 512))], axis=0),
        order,
        preferred_element_type=F32,
    )
    station = (halves[0:1] * 16.0 + halves[16:17]).astype(jnp.int32)
    hot = (rows == station).astype(F32).astype(BF16)
    ordered = pick(split3(delay_in[...]), hot, "right")
    for chunk in range(CHUNKS):
        delay_at[chunk] = ordered[:, chunk * LANES : (chunk + 1) * LANES]
    patches = (
        lax.broadcasted_iota(jnp.int32, (64, 512), 0) == patch_in[...].reshape(1, 512)
    ).astype(F32).astype(BF16)
    ordered = pick(split3(pick(split3(screen_in[...]), hot, "right")), patches, "left")
    for chunk in range(CHUNKS):
        screen_at[chunk] = ordered[:, chunk * LANES : (chunk + 1) * LANES]

    send(1)

    first = (lax.broadcasted_iota(jnp.int32, (8, LANES), 0) * 0 + me * CHANS).astype(F32)

    def freq(k):
        return 50.0 + (first + (k + 0.5)) * STEP

    for k in range(CHANS - 2):
        bend[k] = (2.0 * 150.0 * STEP * STEP) / (freq(k) * freq(k + 1) * freq(k + 2))
    tau = 2.0 * math.pi
    scale = 1.0 / math.sqrt(512.0)
    high = 32

    def fill(i, _):
        chunk = i // 16
        block = i % 16
        j = block // 4
        start = j + 4 * high * (block % 4)
        d = delay_at[chunk, pl.ds(start, high, stride=4), :]
        s = screen_at[chunk, pl.ds(start, high, stride=4), :]
        f0, f1 = freq(0)[0:1], freq(1)[0:1]
        c0, s0 = turn(f0 * d + s * ((150.0 / tau) / f0))
        rc, rs = turn(STEP * d - s * ((150.0 / tau) * STEP / (f0 * f1)))
        wr, wi = c0 * scale, s0 * scale
        here = pl.ds(pl.multiple_of(block * high, high), high)
        for k in range(CHANS):
            weights[k, chunk, here, 0:LANES] = wr.astype(BF16)
            weights[k, chunk, here, LANES : 2 * LANES] = wi.astype(BF16)
            if k < CHANS - 1:
                wr, wi = wr * rc - wi * rs, wr * rs + wi * rc
            if k < CHANS - 2:
                turned = s * bend[k, 0:1, :]
                rc, rs = rc - turned * rs, rs + turned * rc
        return 0

    lax.fori_loop(0, 16 * CHUNKS, fill, 0)

    r = lax.broadcasted_iota(jnp.int32, (256, 256), 0)
    q = lax.broadcasted_iota(jnp.int32, (256, 256), 1)
    apart = (r == (q % PART) * WIDE + q // PART).astype(F32).astype(BF16)
    together = (q == (r % PART) * WIDE + r // PART).astype(F32).astype(BF16)
    lane = lax.broadcasted_iota(jnp.int32, (1, LANES), 1)
    low_half = lane < 64
    even = jnp.bitwise_and(lane, 32) == 0
    own.wait()

    for group in range(GROUPS):
        got[group, DEVICES - 1] = mine_in[:, group]
        for chunk in range(CHUNKS):
            n = PER_CHUNK - (1 if chunk == CHUNKS - 1 else 0)
            landed = got.at[group, pl.ds(chunk * PER_CHUNK, n)]
            pltpu.make_async_copy(landed, landed, volt_recv.at[group, chunk]).wait()
            srcs = WIDE // 4
            for m in range(PER_CHUNK // srcs):
                block = got[group, pl.ds(chunk * PER_CHUNK + srcs * m, srcs)].reshape(256, LANES)
                turned = jnp.dot(apart, block, preferred_element_type=F32)
                other = pltpu.roll(turned, 64, 1)
                other = jnp.where(low_half, other, -other)
                here = WIDE * m
                vperm[:, here : here + WIDE, :] = turned.astype(BF16).reshape(PART, WIDE, LANES)
                vperm[:, LANES + here : LANES + here + WIDE, :] = other.astype(BF16).reshape(PART, WIDE, LANES)

            def beams(step, _):
                for u in range(UNROLL):
                    k = step * UNROLL + u
                    part = jnp.dot(weights[group * PART + k, chunk], vperm[k], preferred_element_type=F32)
                    if chunk == 0:
                        acc[k] = part
                    elif chunk < CHUNKS - 1:
                        acc[k] += part
                    else:
                        total = acc[k] + part
                        sq = (total * total).reshape(4, LANES, LANES)
                        one = jnp.where(low_half, sq[0], sq[2])
                        one += pltpu.roll(jnp.where(low_half, sq[2], sq[0]), 64, 1)
                        two = jnp.where(low_half, sq[1], sq[3])
                        two += pltpu.roll(jnp.where(low_half, sq[3], sq[1]), 64, 1)
                        both = jnp.where(even, one, two)
                        both += jnp.where(even, pltpu.roll(one, 96, 1), pltpu.roll(two, 32, 1))
                        power[k] = (0.25 * both).astype(BF16)
                return 0

            lax.fori_loop(0, PART // UNROLL, beams, 0)

        for m in range(DEVICES // WIDE):
            block = power[:, WIDE * m : WIDE * m + WIDE, :].reshape(256, LANES)
            sent[group, WIDE * m : WIDE * m + WIDE] = (
                jnp.dot(together, block, preferred_element_type=F32).astype(BF16).reshape(WIDE, PART, LANES)
            )
        for offset in OUT_ROUTE[:-1]:
            pltpu.make_async_remote_copy(
                src_ref=sent.at[group, at(owner, offset)],
                dst_ref=back.at[me, group],
                send_sem=out_send.at[group],
                recv_sem=out_recv,
                device_id=at(index, offset),
                device_id_type=LOGICAL,
            ).start()
        back[me, group] = sent[group, at(owner, (0, 0, 0, 0))]

    rest = back.at[pl.ds(0, DEVICES - 1)]
    pltpu.make_async_copy(rest, rest, out_recv).wait()
    eye = (
        lax.broadcasted_iota(jnp.int32, (LANES, LANES), 0) == lax.broadcasted_iota(jnp.int32, (LANES, LANES), 1)
    ).astype(F32).astype(BF16)
    final = lax.dot_general(
        eye, back[...].reshape(DEVICES * CHANS, LANES), (((1,), (1,)), ((), ())), preferred_element_type=F32
    )
    out[...] = final.astype(BF16).reshape(4, 32, DEVICES * CHANS)
    for group in range(GROUPS):
        gone = got.at[group, pl.ds(0, DEVICES - 1)]
        pltpu.make_async_copy(gone, gone, volt_send.at[group]).wait()
        gone = sent.at[group, pl.ds(0, DEVICES - 1)]
        pltpu.make_async_copy(gone, gone, out_send.at[group]).wait()


def body(voltages, station_map, delay, screen, beam_patch):
    table = np.zeros((8, 512), np.int32)
    for k, offset in enumerate(ROUTE):
        table[:4, 4 * k : 4 * k + 4] = np.array(offset, np.int32)[:, None]
    anywhere = pl.BlockSpec(memory_space=pl.ANY)
    return pl.pallas_call(
        kernel,
        out_shape=jax.ShapeDtypeStruct((4, 32, DEVICES * CHANS), BF16),
        in_specs=[anywhere] * 6,
        out_specs=pl.BlockSpec(memory_space=pltpu.VMEM),
        scratch_shapes=[
            pltpu.VMEM((GROUPS, DEVICES, 4, PART, LANES), BF16),
            pltpu.VMEM((4, GROUPS, PART, LANES), BF16),
            pltpu.VMEM((512, 512), F32),
            pltpu.VMEM((64, 512), F32),
            pltpu.VMEM((512,), jnp.int32),
            pltpu.VMEM((512,), jnp.int32),
            pltpu.VMEM((8, 512), jnp.int32),
            pltpu.VMEM((CHUNKS, 512, LANES), F32),
            pltpu.VMEM((CHUNKS, 512, LANES), F32),
            pltpu.VMEM((CHANS, 8, LANES), F32),
            pltpu.VMEM((CHANS, CHUNKS, 512, 2 * LANES), BF16),
            pltpu.VMEM((PART, 2 * LANES, LANES), BF16),
            pltpu.VMEM((PART, 512, LANES), F32),
            pltpu.VMEM((PART, LANES, LANES), BF16),
            pltpu.VMEM((GROUPS, DEVICES, PART, LANES), BF16),
            pltpu.VMEM((DEVICES, GROUPS, PART, LANES), BF16),
            pltpu.SemaphoreType.DMA((5,)),
            pltpu.SemaphoreType.DMA((GROUPS,)),
            pltpu.SemaphoreType.DMA((GROUPS, CHUNKS)),
            pltpu.SemaphoreType.DMA,
            pltpu.SemaphoreType.DMA((GROUPS,)),
            pltpu.SemaphoreType.DMA,
        ],
        compiler_params=pltpu.CompilerParams(collective_id=0, has_side_effects=True, vmem_limit_bytes=56 * 2**20),
        name="beamform",
    )(voltages.reshape(4, DEVICES * GROUPS, PART, LANES), station_map, delay, screen, beam_patch, jnp.asarray(table))


def solution(mesh):
    placed = (P(("chan", "beam"), None, None), P(), P(), P(), P())
    return jax.shard_map(
        body, mesh=mesh, in_specs=placed, out_specs=P(("beam", "chan"), None, None), check_vma=False
    )
```

```python
import math

import jax
import jax.numpy as jnp
import numpy as np
from jax import lax
from jax.experimental import pallas as pl
from jax.experimental.pallas import tpu as pltpu
from jax.sharding import PartitionSpec as P

F32, BF16 = jnp.float32, jnp.bfloat16
LOGICAL = pl.DeviceIdType.LOGICAL
STEP = 300.0 / 2048
DEVICES = 128
CHANS = 16
LANES = 128
CHUNKS = 4
PER_CHUNK = DEVICES // CHUNKS
GROUPS = 2
UNROLL = 8
STEPS = 4
EMIT_AT = CHUNKS - 1
PART = CHANS // GROUPS
WIDE = 256 // PART


def hops(offset):
    return sum(min(a, 4 - a) for a in offset[:3])


def route():
    order = []
    for total in (2, 3, 1, 0):
        quarter = []
        for a in range(4):
            for b in range(4):
                dx, dy = b, (a + b) % 4
                quarter += [(dx, dy, (total - dx - dy) % 4, core) for core in (1, 0)]
        order += sorted(quarter, key=lambda o: -hops(o))
    own = (0, 0, 0, 0)
    return [o for o in order if o != own] + [own]


ROUTE = route()
OUT_ROUTE = sorted(ROUTE, key=lambda o: -hops(o))


def position():
    chan, beam = lax.axis_index("chan"), lax.axis_index("beam")
    return chan // 4, beam % 4, (beam // 4) * 2 + (chan // 2) % 2, chan % 2


def places():
    x, y, z, c = position()
    xs = [(x + d) % 4 for d in range(4)]
    ys = [(y + d) % 4 for d in range(4)]
    zs = [(z + d) % 4 for d in range(4)]
    cs = [(c + d) % 2 for d in range(2)]
    index = ([v * 32 for v in xs], ys, [(v % 2) * 16 + (v // 2) * 4 for v in zs], [v * 8 for v in cs])
    owner = ([v * 4 for v in xs], [v * 16 for v in ys], [(v % 2) * 2 + (v // 2) * 64 for v in zs], cs)
    return index, owner


def at(shares, offset):
    return shares[0][offset[0]] + shares[1][offset[1]] + shares[2][offset[2]] + shares[3][offset[3]]


def fit(fn, odd, terms):
    nodes = (np.cos((2 * np.arange(400) + 1) * np.pi / 800) + 1) / 8
    r = np.sqrt(nodes)
    want = fn(2 * np.pi * r) / (r if odd else 1.0)
    cheb = np.polynomial.chebyshev.Chebyshev.fit(nodes, want, terms - 1, domain=[0, 0.25])
    return [float(v) for v in cheb.convert(kind=np.polynomial.Polynomial).coef]


SIN, COS = fit(np.sin, True, 7), fit(np.cos, False, 8)


def poly(coefs, z):
    total = jnp.full_like(z, coefs[-1])
    for value in coefs[-2::-1]:
        total = total * z + value
    return total


def turn(t):
    r = t - jnp.round(t)
    z = r * r
    return poly(COS, z), r * poly(SIN, z)


def split3(v):
    high = v.astype(BF16)
    rest = v - high.astype(F32)
    mid = rest.astype(BF16)
    low = (rest - mid.astype(F32)).astype(BF16)
    return high, mid, low


def pick(parts, hot, dims):
    total = None
    for part in parts:
        args = (hot, part) if dims == "left" else (part, hot)
        contract = (((0,), (0,)), ((), ())) if dims == "left" else (((1,), (0,)), ((), ()))
        term = lax.dot_general(*args, contract, preferred_element_type=F32)
        total = term if total is None else total + term
    return total


def kernel(
    volt, station_map, delay, screen, beam_patch, offsets, back,
    got, mine_in, delay_in, screen_in, map_in, patch_in, offs_in, delay_at, screen_at, bend, weights, vperm, acc, power,
    sent, load_sem, volt_send, volt_recv, own_sem, out_send, out_recv,
):
    index, owner = places()
    me = at(index, (0, 0, 0, 0))
    x, y, z, c = position()

    loads = [
        pltpu.make_async_copy(src, dst, load_sem.at[i])
        for i, (src, dst) in enumerate(
            [(station_map, map_in), (offsets, offs_in), (delay, delay_in), (screen, screen_in), (beam_patch, patch_in)]
        )
    ]
    for load in loads:
        load.start()
    barrier = pltpu.get_barrier_semaphore()
    for offset in OUT_ROUTE[:-1]:
        pl.semaphore_signal(barrier, inc=1, device_id=at(index, offset), device_id_type=LOGICAL)
    own = pltpu.make_async_copy(volt.at[:, pl.ds(me * GROUPS, GROUPS), :, :], mine_in, own_sem)
    own.start()
    pl.semaphore_wait(barrier, DEVICES - 1)

    def send(group):
        for k, offset in enumerate(ROUTE[:-1]):
            to = at(index, offset)
            pltpu.make_async_remote_copy(
                src_ref=volt.at[:, to * GROUPS + group, :, :],
                dst_ref=got.at[group, k],
                send_sem=volt_send.at[group],
                recv_sem=volt_recv.at[group, k // PER_CHUNK],
                device_id=to,
                device_id_type=LOGICAL,
            ).start()

    send(0)
    for load in loads:
        load.wait()

    col = lax.broadcasted_iota(jnp.int32, (1, 512), 1)
    sx = jnp.bitwise_and(x - offs_in[0:1, :], 3)
    sy = jnp.bitwise_and(y - offs_in[1:2, :], 3)
    sz = jnp.bitwise_and(z - offs_in[2:3, :], 3)
    sc = jnp.bitwise_and(c - offs_in[3:4, :], 1)
    slot = (sx * 32 + sy + jnp.bitwise_and(sz, 1) * 16 + jnp.right_shift(sz, 1) * 4 + sc * 8) * 4
    slot = slot + jnp.bitwise_and(col, 3)
    rows = lax.broadcasted_iota(jnp.int32, (512, 512), 0)
    order = (rows == slot).astype(F32).astype(BF16)
    names = map_in[...].reshape(1, 512)
    tops = jnp.right_shift(names, 4).astype(F32).astype(BF16)
    lows = jnp.bitwise_and(names, 15).astype(F32).astype(BF16)
    halves = jnp.dot(
        jnp.concatenate([jnp.broadcast_to(tops, (16, 512)), jnp.broadcast_to(lows, (16, 512))], axis=0),
        order,
        preferred_element_type=F32,
    )
    station = (halves[0:1] * 16.0 + halves[16:17]).astype(jnp.int32)
    hot = (rows == station).astype(F32).astype(BF16)
    ordered = pick(split3(delay_in[...]), hot, "right")
    for chunk in range(CHUNKS):
        delay_at[chunk] = ordered[:, chunk * LANES : (chunk + 1) * LANES]
    patches = (
        lax.broadcasted_iota(jnp.int32, (64, 512), 0) == patch_in[...].reshape(1, 512)
    ).astype(F32).astype(BF16)
    ordered = pick(split3(pick(split3(screen_in[...]), hot, "right")), patches, "left")
    for chunk in range(CHUNKS):
        screen_at[chunk] = ordered[:, chunk * LANES : (chunk + 1) * LANES]

    send(1)

    first = (lax.broadcasted_iota(jnp.int32, (8, LANES), 0) * 0 + me * CHANS).astype(F32)

    def freq(k):
        return 50.0 + (first + (k + 0.5)) * STEP

    for k in range(CHANS - 2):
        bend[k] = (2.0 * 150.0 * STEP * STEP) / (freq(k) * freq(k + 1) * freq(k + 2))
    tau = 2.0 * math.pi
    scale = 1.0 / math.sqrt(512.0)
    high = 32

    def fill(i, _):
        chunk = i // 16
        block = i % 16
        j = block // 4
        start = j + 4 * high * (block % 4)
        d = delay_at[chunk, pl.ds(start, high, stride=4), :]
        s = screen_at[chunk, pl.ds(start, high, stride=4), :]
        f0, f1 = freq(0)[0:1], freq(1)[0:1]
        c0, s0 = turn(f0 * d + s * ((150.0 / tau) / f0))
        rc, rs = turn(STEP * d - s * ((150.0 / tau) * STEP / (f0 * f1)))
        wr, wi = c0 * scale, s0 * scale
        here = pl.ds(pl.multiple_of(block * high, high), high)
        for k in range(CHANS):
            weights[k, chunk, here, 0:LANES] = wr.astype(BF16)
            weights[k, chunk, here, LANES : 2 * LANES] = wi.astype(BF16)
            if k < CHANS - 1:
                wr, wi = wr * rc - wi * rs, wr * rs + wi * rc
            if k < CHANS - 2:
                turned = s * bend[k, 0:1, :]
                rc, rs = rc - turned * rs, rs + turned * rc
        return 0

    lax.fori_loop(0, 16 * CHUNKS, fill, 0)

    r = lax.broadcasted_iota(jnp.int32, (256, 256), 0)
    q = lax.broadcasted_iota(jnp.int32, (256, 256), 1)
    apart = (r == (q % PART) * WIDE + q // PART).astype(F32).astype(BF16)
    together = (q == (r % PART) * WIDE + r // PART).astype(F32).astype(BF16)
    lane = lax.broadcasted_iota(jnp.int32, (1, LANES), 1)
    low_half = lane < 64
    even = jnp.bitwise_and(lane, 32) == 0
    own.wait()

    def emit(group):
        for offset in OUT_ROUTE[:-1]:
            pltpu.make_async_remote_copy(
                src_ref=sent.at[group, at(owner, offset)],
                dst_ref=back.at[me, group],
                send_sem=out_send.at[group],
                recv_sem=out_recv,
                device_id=at(index, offset),
                device_id_type=LOGICAL,
            ).start()
        keep = pltpu.make_async_copy(sent.at[group, at(owner, (0, 0, 0, 0))], back.at[me, group], own_sem)
        keep.start()
        keep.wait()

    for group in range(GROUPS):
        got[group, DEVICES - 1] = mine_in[:, group]
        for chunk in range(CHUNKS):
            if group and chunk == EMIT_AT:
                emit(group - 1)
            n = PER_CHUNK - (1 if chunk == CHUNKS - 1 else 0)
            landed = got.at[group, pl.ds(chunk * PER_CHUNK, n)]
            pltpu.make_async_copy(landed, landed, volt_recv.at[group, chunk]).wait()
            srcs = WIDE // 4
            for m in range(PER_CHUNK // srcs):
                block = got[group, pl.ds(chunk * PER_CHUNK + srcs * m, srcs)].reshape(256, LANES)
                turned = jnp.dot(apart, block, preferred_element_type=F32)
                other = pltpu.roll(turned, 64, 1)
                other = jnp.where(low_half, other, -other)
                here = WIDE * m
                vperm[:, here : here + WIDE, :] = turned.astype(BF16).reshape(PART, WIDE, LANES)
                vperm[:, LANES + here : LANES + here + WIDE, :] = other.astype(BF16).reshape(PART, WIDE, LANES)

            def beams(step, _):
                for u in range(UNROLL):
                    k = step * UNROLL + u
                    part = jnp.dot(weights[group * PART + k, chunk], vperm[k], preferred_element_type=F32)
                    if chunk == 0:
                        acc[k] = part
                    elif chunk < CHUNKS - 1:
                        acc[k] += part
                    else:
                        total = acc[k] + part
                        sq = (total * total).reshape(4, LANES, LANES)
                        one = jnp.where(low_half, sq[0], sq[2])
                        one += pltpu.roll(jnp.where(low_half, sq[2], sq[0]), 64, 1)
                        two = jnp.where(low_half, sq[1], sq[3])
                        two += pltpu.roll(jnp.where(low_half, sq[3], sq[1]), 64, 1)
                        both = jnp.where(even, one, two)
                        both += jnp.where(even, pltpu.roll(one, 96, 1), pltpu.roll(two, 32, 1))
                        power[k] = (0.25 * both).astype(BF16)
                return 0

            lax.fori_loop(0, PART // UNROLL, beams, 0)

        for m in range(DEVICES // WIDE):
            block = power[:, WIDE * m : WIDE * m + WIDE, :].reshape(256, LANES)
            sent[group, WIDE * m : WIDE * m + WIDE] = (
                jnp.dot(together, block, preferred_element_type=F32).astype(BF16).reshape(WIDE, PART, LANES)
            )
        if group == GROUPS - 1:
            emit(group)

    rest = back.at[pl.ds(0, DEVICES - 1)]
    pltpu.make_async_copy(rest, rest, out_recv).wait()
    for group in range(GROUPS):
        gone = got.at[group, pl.ds(0, DEVICES - 1)]
        pltpu.make_async_copy(gone, gone, volt_send.at[group]).wait()
        gone = sent.at[group, pl.ds(0, DEVICES - 1)]
        pltpu.make_async_copy(gone, gone, out_send.at[group]).wait()


def transpose(rows, out, turned, sems):
    eye = (
        lax.broadcasted_iota(jnp.int32, (LANES, LANES), 0) == lax.broadcasted_iota(jnp.int32, (LANES, LANES), 1)
    ).astype(F32).astype(BF16)
    count = DEVICES * CHANS // STEPS
    copies = []
    for i in range(STEPS):
        block = rows[pl.ds(i * DEVICES // STEPS, DEVICES // STEPS)].reshape(count, LANES)
        final = lax.dot_general(eye, block, (((1,), (1,)), ((), ())), preferred_element_type=F32)
        turned[i] = final.astype(BF16).reshape(4, 32, count)
        copy = pltpu.make_async_copy(turned.at[i], out.at[:, :, pl.ds(i * count, count)], sems.at[i])
        copy.start()
        copies.append(copy)
    for copy in copies:
        copy.wait()


def body(voltages, station_map, delay, screen, beam_patch):
    table = np.zeros((8, 512), np.int32)
    for k, offset in enumerate(ROUTE):
        table[:4, 4 * k : 4 * k + 4] = np.array(offset, np.int32)[:, None]
    anywhere = pl.BlockSpec(memory_space=pl.ANY)
    power = pl.pallas_call(
        kernel,
        out_shape=pltpu.VMEM((DEVICES, GROUPS, PART, LANES), BF16),
        in_specs=[anywhere] * 6,
        out_specs=anywhere,
        scratch_shapes=[
            pltpu.VMEM((GROUPS, DEVICES, 4, PART, LANES), BF16),
            pltpu.VMEM((4, GROUPS, PART, LANES), BF16),
            pltpu.VMEM((512, 512), F32),
            pltpu.VMEM((64, 512), F32),
            pltpu.VMEM((512,), jnp.int32),
            pltpu.VMEM((512,), jnp.int32),
            pltpu.VMEM((8, 512), jnp.int32),
            pltpu.VMEM((CHUNKS, 512, LANES), F32),
            pltpu.VMEM((CHUNKS, 512, LANES), F32),
            pltpu.VMEM((CHANS, 8, LANES), F32),
            pltpu.VMEM((CHANS, CHUNKS, 512, 2 * LANES), BF16),
            pltpu.VMEM((PART, 2 * LANES, LANES), BF16),
            pltpu.VMEM((PART, 512, LANES), F32),
            pltpu.VMEM((PART, LANES, LANES), BF16),
            pltpu.VMEM((GROUPS, DEVICES, PART, LANES), BF16),
            pltpu.SemaphoreType.DMA((5,)),
            pltpu.SemaphoreType.DMA((GROUPS,)),
            pltpu.SemaphoreType.DMA((GROUPS, CHUNKS)),
            pltpu.SemaphoreType.DMA,
            pltpu.SemaphoreType.DMA((GROUPS,)),
            pltpu.SemaphoreType.DMA,
        ],
        compiler_params=pltpu.CompilerParams(collective_id=0, has_side_effects=True, vmem_limit_bytes=56 * 2**20),
        name="beamform",
    )(voltages.reshape(4, DEVICES * GROUPS, PART, LANES), station_map, delay, screen, beam_patch, jnp.asarray(table))
    return pl.pallas_call(
        transpose,
        out_shape=jax.ShapeDtypeStruct((4, 32, DEVICES * CHANS), BF16),
        in_specs=[pl.BlockSpec(memory_space=pltpu.VMEM)],
        out_specs=anywhere,
        scratch_shapes=[
            pltpu.VMEM((STEPS, 4, 32, DEVICES * CHANS // STEPS), BF16),
            pltpu.SemaphoreType.DMA((STEPS,)),
        ],
        name="transpose",
    )(pltpu.with_memory_space_constraint(power, pltpu.VMEM))


def solution(mesh):
    placed = (P(("chan", "beam"), None, None), P(), P(), P(), P())
    return jax.shard_map(
        body, mesh=mesh, in_specs=placed, out_specs=P(("beam", "chan"), None, None), check_vma=False
    )
```

```python
import math

import jax
import jax.numpy as jnp
import numpy as np
from jax import lax
from jax.experimental import pallas as pl
from jax.experimental.pallas import tpu as pltpu
from jax.sharding import PartitionSpec as P

F32, BF16 = jnp.float32, jnp.bfloat16
LOGICAL = pl.DeviceIdType.LOGICAL
STEP = 300.0 / 2048
DEVICES = 128
CHANS = 16
LANES = 128
CHUNKS = 4
PER_CHUNK = DEVICES // CHUNKS
GROUPS = 2
UNROLL = 8
STEPS = 4
EMIT_AT = CHUNKS - 1
PART = CHANS // GROUPS
WIDE = 256 // PART


def hops(offset):
    return sum(min(a, 4 - a) for a in offset[:3])


def route():
    lines = [(0, 0, 0)] + [tuple(d * (axis == i) for i in range(3)) for d in (2, 1, 3) for axis in range(3)]
    planes, rest = [], []
    for i in range(9):
        u, v = i % 3 + 1, (i + i // 3) % 3 + 1
        planes += [(u, v, 0), (0, u, v), (v, 0, u)]
    for i in range(27):
        rest.append((i % 3 + 1, (i + i // 3) % 3 + 1, (i + i // 9) % 3 + 1))
    every = [chip + (core,) for chip in lines + planes + rest for core in (1, 0)]
    own = (0, 0, 0, 0)
    return [o for o in every if o != own] + [own]


LINES, PLANES = 19, 54
ROUTE = route()
OUT_ROUTE = sorted(ROUTE, key=lambda o: -hops(o))


def position():
    chan, beam = lax.axis_index("chan"), lax.axis_index("beam")
    return chan // 4, beam % 4, (beam // 4) * 2 + (chan // 2) % 2, chan % 2


def places():
    x, y, z, c = position()
    xs = [(x + d) % 4 for d in range(4)]
    ys = [(y + d) % 4 for d in range(4)]
    zs = [(z + d) % 4 for d in range(4)]
    cs = [(c + d) % 2 for d in range(2)]
    index = ([v * 32 for v in xs], ys, [(v % 2) * 16 + (v // 2) * 4 for v in zs], [v * 8 for v in cs])
    owner = ([v * 4 for v in xs], [v * 16 for v in ys], [(v % 2) * 2 + (v // 2) * 64 for v in zs], cs)
    return index, owner


def at(shares, offset):
    return shares[0][offset[0]] + shares[1][offset[1]] + shares[2][offset[2]] + shares[3][offset[3]]


def fit(fn, odd, terms):
    nodes = (np.cos((2 * np.arange(400) + 1) * np.pi / 800) + 1) / 8
    r = np.sqrt(nodes)
    want = fn(2 * np.pi * r) / (r if odd else 1.0)
    cheb = np.polynomial.chebyshev.Chebyshev.fit(nodes, want, terms - 1, domain=[0, 0.25])
    return [float(v) for v in cheb.convert(kind=np.polynomial.Polynomial).coef]


SIN, COS = fit(np.sin, True, 7), fit(np.cos, False, 8)


def poly(coefs, z):
    total = jnp.full_like(z, coefs[-1])
    for value in coefs[-2::-1]:
        total = total * z + value
    return total


def turn(t):
    r = t - jnp.round(t)
    z = r * r
    return poly(COS, z), r * poly(SIN, z)


def split3(v):
    high = v.astype(BF16)
    rest = v - high.astype(F32)
    mid = rest.astype(BF16)
    low = (rest - mid.astype(F32)).astype(BF16)
    return high, mid, low


def pick(parts, hot, dims):
    total = None
    for part in parts:
        args = (hot, part) if dims == "left" else (part, hot)
        contract = (((0,), (0,)), ((), ())) if dims == "left" else (((1,), (0,)), ((), ()))
        term = lax.dot_general(*args, contract, preferred_element_type=F32)
        total = term if total is None else total + term
    return total


def kernel(
    volt, station_map, delay, screen, beam_patch, offsets, back,
    got, mine_in, delay_in, screen_in, map_in, patch_in, offs_in, delay_at, screen_at, bend, weights, vperm, acc, power,
    sent, load_sem, volt_send, volt_recv, own_sem, lines_in, planes_in, out_send, out_recv,
):
    index, owner = places()
    me = at(index, (0, 0, 0, 0))
    x, y, z, c = position()

    loads = [
        pltpu.make_async_copy(src, dst, load_sem.at[i])
        for i, (src, dst) in enumerate(
            [(station_map, map_in), (offsets, offs_in), (delay, delay_in), (screen, screen_in), (beam_patch, patch_in)]
        )
    ]
    for load in loads:
        load.start()
    barrier = pltpu.get_barrier_semaphore()
    for offset in ROUTE[:LINES]:
        pl.semaphore_signal(barrier, inc=1, device_id=at(index, offset), device_id_type=LOGICAL)
    own = pltpu.make_async_copy(volt.at[:, pl.ds(me * GROUPS, GROUPS), :, :], mine_in, own_sem)
    own.start()
    pl.semaphore_wait(barrier, LINES)

    def send(group, first, last):
        for k, offset in enumerate(ROUTE):
            if not first <= k < last:
                continue
            to = at(index, offset)
            pltpu.make_async_remote_copy(
                src_ref=volt.at[:, to * GROUPS + group, :, :],
                dst_ref=got.at[group, k],
                send_sem=volt_send.at[group],
                recv_sem=volt_recv.at[group, k // PER_CHUNK],
                device_id=to,
                device_id_type=LOGICAL,
            ).start()

    for d in (2, 1, 3):
        for offset in ((d, 0, 0, 0), (0, d, 0, 0)):
            pl.semaphore_signal(lines_in, inc=1, device_id=at(index, offset), device_id_type=LOGICAL)
    send(0, 0, LINES)
    pl.semaphore_wait(lines_in, 6)
    for d in (2, 1, 3):
        pl.semaphore_signal(planes_in, inc=1, device_id=at(index, (d, 0, 0, 0)), device_id_type=LOGICAL)
    send(0, LINES, LINES + PLANES)
    for load in loads:
        load.wait()

    col = lax.broadcasted_iota(jnp.int32, (1, 512), 1)
    sx = jnp.bitwise_and(x - offs_in[0:1, :], 3)
    sy = jnp.bitwise_and(y - offs_in[1:2, :], 3)
    sz = jnp.bitwise_and(z - offs_in[2:3, :], 3)
    sc = jnp.bitwise_and(c - offs_in[3:4, :], 1)
    slot = (sx * 32 + sy + jnp.bitwise_and(sz, 1) * 16 + jnp.right_shift(sz, 1) * 4 + sc * 8) * 4
    slot = slot + jnp.bitwise_and(col, 3)
    rows = lax.broadcasted_iota(jnp.int32, (512, 512), 0)
    order = (rows == slot).astype(F32).astype(BF16)
    names = map_in[...].reshape(1, 512)
    tops = jnp.right_shift(names, 4).astype(F32).astype(BF16)
    lows = jnp.bitwise_and(names, 15).astype(F32).astype(BF16)
    halves = jnp.dot(
        jnp.concatenate([jnp.broadcast_to(tops, (16, 512)), jnp.broadcast_to(lows, (16, 512))], axis=0),
        order,
        preferred_element_type=F32,
    )
    station = (halves[0:1] * 16.0 + halves[16:17]).astype(jnp.int32)
    hot = (rows == station).astype(F32).astype(BF16)
    ordered = pick(split3(delay_in[...]), hot, "right")
    for chunk in range(CHUNKS):
        delay_at[chunk] = ordered[:, chunk * LANES : (chunk + 1) * LANES]
    patches = (
        lax.broadcasted_iota(jnp.int32, (64, 512), 0) == patch_in[...].reshape(1, 512)
    ).astype(F32).astype(BF16)
    ordered = pick(split3(pick(split3(screen_in[...]), hot, "right")), patches, "left")
    for chunk in range(CHUNKS):
        screen_at[chunk] = ordered[:, chunk * LANES : (chunk + 1) * LANES]

    pl.semaphore_wait(planes_in, 3)
    send(0, LINES + PLANES, DEVICES - 1)
    send(1, 0, DEVICES - 1)

    first = (lax.broadcasted_iota(jnp.int32, (8, LANES), 0) * 0 + me * CHANS).astype(F32)

    def freq(k):
        return 50.0 + (first + (k + 0.5)) * STEP

    for k in range(CHANS - 2):
        bend[k] = (2.0 * 150.0 * STEP * STEP) / (freq(k) * freq(k + 1) * freq(k + 2))
    tau = 2.0 * math.pi
    scale = 1.0 / math.sqrt(512.0)
    high = 32

    def fill(i, _):
        chunk = i // 16
        block = i % 16
        j = block // 4
        start = j + 4 * high * (block % 4)
        d = delay_at[chunk, pl.ds(start, high, stride=4), :]
        s = screen_at[chunk, pl.ds(start, high, stride=4), :]
        f0, f1 = freq(0)[0:1], freq(1)[0:1]
        c0, s0 = turn(f0 * d + s * ((150.0 / tau) / f0))
        rc, rs = turn(STEP * d - s * ((150.0 / tau) * STEP / (f0 * f1)))
        wr, wi = c0 * scale, s0 * scale
        here = pl.ds(pl.multiple_of(block * high, high), high)
        for k in range(CHANS):
            weights[k, chunk, here, 0:LANES] = wr.astype(BF16)
            weights[k, chunk, here, LANES : 2 * LANES] = wi.astype(BF16)
            if k < CHANS - 1:
                wr, wi = wr * rc - wi * rs, wr * rs + wi * rc
            if k < CHANS - 2:
                turned = s * bend[k, 0:1, :]
                rc, rs = rc - turned * rs, rs + turned * rc
        return 0

    lax.fori_loop(0, 16 * CHUNKS, fill, 0)

    r = lax.broadcasted_iota(jnp.int32, (256, 256), 0)
    q = lax.broadcasted_iota(jnp.int32, (256, 256), 1)
    apart = (r == (q % PART) * WIDE + q // PART).astype(F32).astype(BF16)
    together = (q == (r % PART) * WIDE + r // PART).astype(F32).astype(BF16)
    lane = lax.broadcasted_iota(jnp.int32, (1, LANES), 1)
    low_half = lane < 64
    even = jnp.bitwise_and(lane, 32) == 0
    own.wait()

    def emit(group):
        for offset in OUT_ROUTE[:-1]:
            pltpu.make_async_remote_copy(
                src_ref=sent.at[group, at(owner, offset)],
                dst_ref=back.at[me, group],
                send_sem=out_send.at[group],
                recv_sem=out_recv,
                device_id=at(index, offset),
                device_id_type=LOGICAL,
            ).start()
        keep = pltpu.make_async_copy(sent.at[group, at(owner, (0, 0, 0, 0))], back.at[me, group], own_sem)
        keep.start()
        keep.wait()

    for group in range(GROUPS):
        got[group, DEVICES - 1] = mine_in[:, group]
        for chunk in range(CHUNKS):
            if group and chunk == EMIT_AT:
                emit(group - 1)
            n = PER_CHUNK - (1 if chunk == CHUNKS - 1 else 0)
            landed = got.at[group, pl.ds(chunk * PER_CHUNK, n)]
            pltpu.make_async_copy(landed, landed, volt_recv.at[group, chunk]).wait()
            srcs = WIDE // 4
            for m in range(PER_CHUNK // srcs):
                block = got[group, pl.ds(chunk * PER_CHUNK + srcs * m, srcs)].reshape(256, LANES)
                turned = jnp.dot(apart, block, preferred_element_type=F32)
                other = pltpu.roll(turned, 64, 1)
                other = jnp.where(low_half, other, -other)
                here = WIDE * m
                vperm[:, here : here + WIDE, :] = turned.astype(BF16).reshape(PART, WIDE, LANES)
                vperm[:, LANES + here : LANES + here + WIDE, :] = other.astype(BF16).reshape(PART, WIDE, LANES)

            def beams(step, _):
                for u in range(UNROLL):
                    k = step * UNROLL + u
                    part = jnp.dot(weights[group * PART + k, chunk], vperm[k], preferred_element_type=F32)
                    if chunk == 0:
                        acc[k] = part
                    elif chunk < CHUNKS - 1:
                        acc[k] += part
                    else:
                        total = acc[k] + part
                        sq = (total * total).reshape(4, LANES, LANES)
                        one = jnp.where(low_half, sq[0], sq[2])
                        one += pltpu.roll(jnp.where(low_half, sq[2], sq[0]), 64, 1)
                        two = jnp.where(low_half, sq[1], sq[3])
                        two += pltpu.roll(jnp.where(low_half, sq[3], sq[1]), 64, 1)
                        both = jnp.where(even, one, two)
                        both += jnp.where(even, pltpu.roll(one, 96, 1), pltpu.roll(two, 32, 1))
                        power[k] = (0.25 * both).astype(BF16)
                return 0

            lax.fori_loop(0, PART // UNROLL, beams, 0)

        for m in range(DEVICES // WIDE):
            block = power[:, WIDE * m : WIDE * m + WIDE, :].reshape(256, LANES)
            sent[group, WIDE * m : WIDE * m + WIDE] = (
                jnp.dot(together, block, preferred_element_type=F32).astype(BF16).reshape(WIDE, PART, LANES)
            )
        if group == GROUPS - 1:
            emit(group)

    rest = back.at[pl.ds(0, DEVICES - 1)]
    pltpu.make_async_copy(rest, rest, out_recv).wait()
    for group in range(GROUPS):
        gone = got.at[group, pl.ds(0, DEVICES - 1)]
        pltpu.make_async_copy(gone, gone, volt_send.at[group]).wait()
        gone = sent.at[group, pl.ds(0, DEVICES - 1)]
        pltpu.make_async_copy(gone, gone, out_send.at[group]).wait()


def transpose(rows, out, turned, sems):
    eye = (
        lax.broadcasted_iota(jnp.int32, (LANES, LANES), 0) == lax.broadcasted_iota(jnp.int32, (LANES, LANES), 1)
    ).astype(F32).astype(BF16)
    count = DEVICES * CHANS // STEPS
    copies = []
    for i in range(STEPS):
        block = rows[pl.ds(i * DEVICES // STEPS, DEVICES // STEPS)].reshape(count, LANES)
        final = lax.dot_general(eye, block, (((1,), (1,)), ((), ())), preferred_element_type=F32)
        turned[i] = final.astype(BF16).reshape(4, 32, count)
        copy = pltpu.make_async_copy(turned.at[i], out.at[:, :, pl.ds(i * count, count)], sems.at[i])
        copy.start()
        copies.append(copy)
    for copy in copies:
        copy.wait()


def body(voltages, station_map, delay, screen, beam_patch):
    table = np.zeros((8, 512), np.int32)
    for k, offset in enumerate(ROUTE):
        table[:4, 4 * k : 4 * k + 4] = np.array(offset, np.int32)[:, None]
    anywhere = pl.BlockSpec(memory_space=pl.ANY)
    power = pl.pallas_call(
        kernel,
        out_shape=pltpu.VMEM((DEVICES, GROUPS, PART, LANES), BF16),
        in_specs=[anywhere] * 6,
        out_specs=anywhere,
        scratch_shapes=[
            pltpu.VMEM((GROUPS, DEVICES, 4, PART, LANES), BF16),
            pltpu.VMEM((4, GROUPS, PART, LANES), BF16),
            pltpu.VMEM((512, 512), F32),
            pltpu.VMEM((64, 512), F32),
            pltpu.VMEM((512,), jnp.int32),
            pltpu.VMEM((512,), jnp.int32),
            pltpu.VMEM((8, 512), jnp.int32),
            pltpu.VMEM((CHUNKS, 512, LANES), F32),
            pltpu.VMEM((CHUNKS, 512, LANES), F32),
            pltpu.VMEM((CHANS, 8, LANES), F32),
            pltpu.VMEM((CHANS, CHUNKS, 512, 2 * LANES), BF16),
            pltpu.VMEM((PART, 2 * LANES, LANES), BF16),
            pltpu.VMEM((PART, 512, LANES), F32),
            pltpu.VMEM((PART, LANES, LANES), BF16),
            pltpu.VMEM((GROUPS, DEVICES, PART, LANES), BF16),
            pltpu.SemaphoreType.DMA((5,)),
            pltpu.SemaphoreType.DMA((GROUPS,)),
            pltpu.SemaphoreType.DMA((GROUPS, CHUNKS)),
            pltpu.SemaphoreType.DMA,
            pltpu.SemaphoreType.REGULAR,
            pltpu.SemaphoreType.REGULAR,
            pltpu.SemaphoreType.DMA((GROUPS,)),
            pltpu.SemaphoreType.DMA,
        ],
        compiler_params=pltpu.CompilerParams(collective_id=0, has_side_effects=True, vmem_limit_bytes=56 * 2**20),
        name="beamform",
    )(voltages.reshape(4, DEVICES * GROUPS, PART, LANES), station_map, delay, screen, beam_patch, jnp.asarray(table))
    return pl.pallas_call(
        transpose,
        out_shape=jax.ShapeDtypeStruct((4, 32, DEVICES * CHANS), BF16),
        in_specs=[pl.BlockSpec(memory_space=pltpu.VMEM)],
        out_specs=anywhere,
        scratch_shapes=[
            pltpu.VMEM((STEPS, 4, 32, DEVICES * CHANS // STEPS), BF16),
            pltpu.SemaphoreType.DMA((STEPS,)),
        ],
        name="transpose",
    )(pltpu.with_memory_space_constraint(power, pltpu.VMEM))


def solution(mesh):
    placed = (P(("chan", "beam"), None, None), P(), P(), P(), P())
    return jax.shard_map(
        body, mesh=mesh, in_specs=placed, out_specs=P(("beam", "chan"), None, None), check_vma=False
    )
```

```python
import math

import jax
import jax.numpy as jnp
import numpy as np
from jax import lax
from jax.experimental import pallas as pl
from jax.experimental.pallas import tpu as pltpu
from jax.sharding import PartitionSpec as P

F32, BF16 = jnp.float32, jnp.bfloat16
LOGICAL = pl.DeviceIdType.LOGICAL
STEP = 300.0 / 2048
DEVICES = 128
CHANS = 16
LANES = 128
CHUNKS = 4
PER_CHUNK = DEVICES // CHUNKS
GROUPS = 2
UNROLL = 8
STEPS = 4
EMIT_AT = CHUNKS - 1
PART = CHANS // GROUPS
WIDE = 256 // PART


def hops(offset):
    return sum(min(a, 4 - a) for a in offset[:3])


def route():
    lines = [(0, 0, 0)] + [tuple(d * (axis == i) for i in range(3)) for d in (2, 1, 3) for axis in range(3)]
    planes, rest = [], []
    for i in range(9):
        u, v = i % 3 + 1, (i + i // 3) % 3 + 1
        planes += [(u, v, 0), (0, u, v), (v, 0, u)]
    for i in range(27):
        rest.append((i % 3 + 1, (i + i // 3) % 3 + 1, (i + i // 9) % 3 + 1))
    every = [chip + (core,) for chip in lines + planes + rest for core in (1, 0)]
    own = (0, 0, 0, 0)
    return [o for o in every if o != own] + [own]


LINES, PLANES = 19, 54
ROUTE = route()
OUT_ROUTE = sorted(ROUTE, key=lambda o: -hops(o))


def position():
    chan, beam = lax.axis_index("chan"), lax.axis_index("beam")
    return chan // 4, beam % 4, (beam // 4) * 2 + (chan // 2) % 2, chan % 2


def places():
    x, y, z, c = position()
    xs = [(x + d) % 4 for d in range(4)]
    ys = [(y + d) % 4 for d in range(4)]
    zs = [(z + d) % 4 for d in range(4)]
    cs = [(c + d) % 2 for d in range(2)]
    index = ([v * 32 for v in xs], ys, [(v % 2) * 16 + (v // 2) * 4 for v in zs], [v * 8 for v in cs])
    owner = ([v * 4 for v in xs], [v * 16 for v in ys], [(v % 2) * 2 + (v // 2) * 64 for v in zs], cs)
    return index, owner


def at(shares, offset):
    return shares[0][offset[0]] + shares[1][offset[1]] + shares[2][offset[2]] + shares[3][offset[3]]


def fit(fn, odd, terms):
    nodes = (np.cos((2 * np.arange(400) + 1) * np.pi / 800) + 1) / 8
    r = np.sqrt(nodes)
    want = fn(2 * np.pi * r) / (r if odd else 1.0)
    cheb = np.polynomial.chebyshev.Chebyshev.fit(nodes, want, terms - 1, domain=[0, 0.25])
    return [float(v) for v in cheb.convert(kind=np.polynomial.Polynomial).coef]


SIN, COS = fit(np.sin, True, 7), fit(np.cos, False, 8)


def poly(coefs, z):
    total = jnp.full_like(z, coefs[-1])
    for value in coefs[-2::-1]:
        total = total * z + value
    return total


def turn(t):
    r = t - jnp.round(t)
    z = r * r
    return poly(COS, z), r * poly(SIN, z)


def split3(v):
    high = v.astype(BF16)
    rest = v - high.astype(F32)
    mid = rest.astype(BF16)
    low = (rest - mid.astype(F32)).astype(BF16)
    return high, mid, low


def pick(parts, hot, dims):
    total = None
    for part in parts:
        args = (hot, part) if dims == "left" else (part, hot)
        contract = (((0,), (0,)), ((), ())) if dims == "left" else (((1,), (0,)), ((), ()))
        term = lax.dot_general(*args, contract, preferred_element_type=F32)
        total = term if total is None else total + term
    return total


def kernel(
    volt, station_map, delay, screen, beam_patch, offsets, back,
    got, mine_in, delay_in, screen_in, map_in, patch_in, offs_in, delay_at, screen_at, bend, weights, vperm, acc, power,
    sent, load_sem, volt_send, volt_recv, own_sem, keep_sem, lines_in, planes_in, out_send, out_recv,
):
    index, owner = places()
    me = at(index, (0, 0, 0, 0))
    x, y, z, c = position()

    barrier = pltpu.get_barrier_semaphore()
    for offset in ROUTE[:LINES]:
        pl.semaphore_signal(barrier, inc=1, device_id=at(index, offset), device_id_type=LOGICAL)
    loads = [
        pltpu.make_async_copy(src, dst, load_sem.at[i])
        for i, (src, dst) in enumerate(
            [(station_map, map_in), (offsets, offs_in), (delay, delay_in), (screen, screen_in), (beam_patch, patch_in)]
        )
    ]
    for load in loads:
        load.start()
    own = pltpu.make_async_copy(volt.at[:, pl.ds(me * GROUPS, GROUPS), :, :], mine_in, own_sem)
    own.start()
    pl.semaphore_wait(barrier, LINES)

    def send(group, first, last):
        for k, offset in enumerate(ROUTE):
            if not first <= k < last:
                continue
            to = at(index, offset)
            pltpu.make_async_remote_copy(
                src_ref=volt.at[:, to * GROUPS + group, :, :],
                dst_ref=got.at[group, k],
                send_sem=volt_send.at[group],
                recv_sem=volt_recv.at[group, k // PER_CHUNK],
                device_id=to,
                device_id_type=LOGICAL,
            ).start()

    for d in (2, 1, 3):
        for offset in ((d, 0, 0, 0), (0, d, 0, 0)):
            pl.semaphore_signal(lines_in, inc=1, device_id=at(index, offset), device_id_type=LOGICAL)
    send(0, 0, LINES)
    pl.semaphore_wait(lines_in, 6)
    for d in (2, 1, 3):
        pl.semaphore_signal(planes_in, inc=1, device_id=at(index, (d, 0, 0, 0)), device_id_type=LOGICAL)
    send(0, LINES, LINES + PLANES)
    for load in loads:
        load.wait()

    col = lax.broadcasted_iota(jnp.int32, (1, 512), 1)
    sx = jnp.bitwise_and(x - offs_in[0:1, :], 3)
    sy = jnp.bitwise_and(y - offs_in[1:2, :], 3)
    sz = jnp.bitwise_and(z - offs_in[2:3, :], 3)
    sc = jnp.bitwise_and(c - offs_in[3:4, :], 1)
    slot = (sx * 32 + sy + jnp.bitwise_and(sz, 1) * 16 + jnp.right_shift(sz, 1) * 4 + sc * 8) * 4
    slot = slot + jnp.bitwise_and(col, 3)
    rows = lax.broadcasted_iota(jnp.int32, (512, 512), 0)
    order = (rows == slot).astype(F32).astype(BF16)
    names = map_in[...].reshape(1, 512)
    tops = jnp.right_shift(names, 4).astype(F32).astype(BF16)
    lows = jnp.bitwise_and(names, 15).astype(F32).astype(BF16)
    halves = jnp.dot(
        jnp.concatenate([jnp.broadcast_to(tops, (16, 512)), jnp.broadcast_to(lows, (16, 512))], axis=0),
        order,
        preferred_element_type=F32,
    )
    station = (halves[0:1] * 16.0 + halves[16:17]).astype(jnp.int32)
    hot = (rows == station).astype(F32).astype(BF16)
    ordered = pick(split3(delay_in[...]), hot, "right")
    for chunk in range(CHUNKS):
        delay_at[chunk] = ordered[:, chunk * LANES : (chunk + 1) * LANES]
    patches = (
        lax.broadcasted_iota(jnp.int32, (64, 512), 0) == patch_in[...].reshape(1, 512)
    ).astype(F32).astype(BF16)
    ordered = pick(split3(pick(split3(screen_in[...]), hot, "right")), patches, "left")
    for chunk in range(CHUNKS):
        screen_at[chunk] = ordered[:, chunk * LANES : (chunk + 1) * LANES]

    pl.semaphore_wait(planes_in, 3)
    send(0, LINES + PLANES, DEVICES - 1)
    send(1, 0, DEVICES - 1)

    first = (lax.broadcasted_iota(jnp.int32, (8, LANES), 0) * 0 + me * CHANS).astype(F32)

    def freq(k):
        return 50.0 + (first + (k + 0.5)) * STEP

    for k in range(CHANS - 2):
        bend[k] = (2.0 * 150.0 * STEP * STEP) / (freq(k) * freq(k + 1) * freq(k + 2))
    tau = 2.0 * math.pi
    scale = 1.0 / math.sqrt(512.0)
    high = 32

    def fill(i, _):
        chunk = i // 16
        block = i % 16
        j = block // 4
        start = j + 4 * high * (block % 4)
        d = delay_at[chunk, pl.ds(start, high, stride=4), :]
        s = screen_at[chunk, pl.ds(start, high, stride=4), :]
        f0, f1 = freq(0)[0:1], freq(1)[0:1]
        c0, s0 = turn(f0 * d + s * ((150.0 / tau) / f0))
        rc, rs = turn(STEP * d - s * ((150.0 / tau) * STEP / (f0 * f1)))
        wr, wi = c0 * scale, s0 * scale
        here = pl.ds(pl.multiple_of(block * high, high), high)
        for k in range(CHANS):
            weights[k, chunk, here, 0:LANES] = wr.astype(BF16)
            weights[k, chunk, here, LANES : 2 * LANES] = wi.astype(BF16)
            if k < CHANS - 1:
                wr, wi = wr * rc - wi * rs, wr * rs + wi * rc
            if k < CHANS - 2:
                turned = s * bend[k, 0:1, :]
                rc, rs = rc - turned * rs, rs + turned * rc
        return 0

    lax.fori_loop(0, 16 * CHUNKS, fill, 0)

    r = lax.broadcasted_iota(jnp.int32, (256, 256), 0)
    q = lax.broadcasted_iota(jnp.int32, (256, 256), 1)
    apart = (r == (q % PART) * WIDE + q // PART).astype(F32).astype(BF16)
    together = (q == (r % PART) * WIDE + r // PART).astype(F32).astype(BF16)
    lane = lax.broadcasted_iota(jnp.int32, (1, LANES), 1)
    low_half = lane < 64
    even = jnp.bitwise_and(lane, 32) == 0
    own.wait()

    kept = []

    def emit(group):
        for offset in OUT_ROUTE[:-1]:
            pltpu.make_async_remote_copy(
                src_ref=sent.at[group, at(owner, offset)],
                dst_ref=back.at[me, group],
                send_sem=out_send.at[group],
                recv_sem=out_recv,
                device_id=at(index, offset),
                device_id_type=LOGICAL,
            ).start()
        keep = pltpu.make_async_copy(sent.at[group, at(owner, (0, 0, 0, 0))], back.at[me, group], keep_sem.at[group])
        keep.start()
        kept.append(keep)

    for group in range(GROUPS):
        got[group, DEVICES - 1] = mine_in[:, group]
        for chunk in range(CHUNKS):
            if group and chunk == EMIT_AT:
                emit(group - 1)
            n = PER_CHUNK - (1 if chunk == CHUNKS - 1 else 0)
            landed = got.at[group, pl.ds(chunk * PER_CHUNK, n)]
            pltpu.make_async_copy(landed, landed, volt_recv.at[group, chunk]).wait()
            srcs = WIDE // 4
            for m in range(PER_CHUNK // srcs):
                block = got[group, pl.ds(chunk * PER_CHUNK + srcs * m, srcs)].reshape(256, LANES)
                turned = jnp.dot(apart, block, preferred_element_type=F32)
                other = pltpu.roll(turned, 64, 1)
                other = jnp.where(low_half, other, -other)
                here = WIDE * m
                vperm[:, here : here + WIDE, :] = turned.astype(BF16).reshape(PART, WIDE, LANES)
                vperm[:, LANES + here : LANES + here + WIDE, :] = other.astype(BF16).reshape(PART, WIDE, LANES)

            def beams(step, _):
                for u in range(UNROLL):
                    k = step * UNROLL + u
                    part = jnp.dot(weights[group * PART + k, chunk], vperm[k], preferred_element_type=F32)
                    if chunk == 0:
                        acc[k] = part
                    elif chunk < CHUNKS - 1:
                        acc[k] += part
                    else:
                        total = acc[k] + part
                        sq = (total * total).reshape(4, LANES, LANES)
                        one = jnp.where(low_half, sq[0], sq[2])
                        one += pltpu.roll(jnp.where(low_half, sq[2], sq[0]), 64, 1)
                        two = jnp.where(low_half, sq[1], sq[3])
                        two += pltpu.roll(jnp.where(low_half, sq[3], sq[1]), 64, 1)
                        both = jnp.where(even, one, two)
                        both += jnp.where(even, pltpu.roll(one, 96, 1), pltpu.roll(two, 32, 1))
                        power[k] = (0.25 * both).astype(BF16)
                return 0

            lax.fori_loop(0, PART // UNROLL, beams, 0)

        for m in range(DEVICES // WIDE):
            block = power[:, WIDE * m : WIDE * m + WIDE, :].reshape(256, LANES)
            sent[group, WIDE * m : WIDE * m + WIDE] = (
                jnp.dot(together, block, preferred_element_type=F32).astype(BF16).reshape(WIDE, PART, LANES)
            )
        if group == GROUPS - 1:
            emit(group)

    for keep in kept:
        keep.wait()
    rest = back.at[pl.ds(0, DEVICES - 1)]
    pltpu.make_async_copy(rest, rest, out_recv).wait()
    for group in range(GROUPS):
        gone = got.at[group, pl.ds(0, DEVICES - 1)]
        pltpu.make_async_copy(gone, gone, volt_send.at[group]).wait()
        gone = sent.at[group, pl.ds(0, DEVICES - 1)]
        pltpu.make_async_copy(gone, gone, out_send.at[group]).wait()


def transpose(rows, out, turned, sems):
    eye = (
        lax.broadcasted_iota(jnp.int32, (LANES, LANES), 0) == lax.broadcasted_iota(jnp.int32, (LANES, LANES), 1)
    ).astype(F32).astype(BF16)
    count = DEVICES * CHANS // STEPS
    copies = []
    for i in range(STEPS):
        block = rows[pl.ds(i * DEVICES // STEPS, DEVICES // STEPS)].reshape(count, LANES)
        final = lax.dot_general(eye, block, (((1,), (1,)), ((), ())), preferred_element_type=F32)
        turned[i] = final.astype(BF16).reshape(4, 32, count)
        copy = pltpu.make_async_copy(turned.at[i], out.at[:, :, pl.ds(i * count, count)], sems.at[i])
        copy.start()
        copies.append(copy)
    for copy in copies:
        copy.wait()


def body(voltages, station_map, delay, screen, beam_patch):
    table = np.zeros((8, 512), np.int32)
    for k, offset in enumerate(ROUTE):
        table[:4, 4 * k : 4 * k + 4] = np.array(offset, np.int32)[:, None]
    anywhere = pl.BlockSpec(memory_space=pl.ANY)
    power = pl.pallas_call(
        kernel,
        out_shape=pltpu.VMEM((DEVICES, GROUPS, PART, LANES), BF16),
        in_specs=[anywhere] * 6,
        out_specs=anywhere,
        scratch_shapes=[
            pltpu.VMEM((GROUPS, DEVICES, 4, PART, LANES), BF16),
            pltpu.VMEM((4, GROUPS, PART, LANES), BF16),
            pltpu.VMEM((512, 512), F32),
            pltpu.VMEM((64, 512), F32),
            pltpu.VMEM((512,), jnp.int32),
            pltpu.VMEM((512,), jnp.int32),
            pltpu.VMEM((8, 512), jnp.int32),
            pltpu.VMEM((CHUNKS, 512, LANES), F32),
            pltpu.VMEM((CHUNKS, 512, LANES), F32),
            pltpu.VMEM((CHANS, 8, LANES), F32),
            pltpu.VMEM((CHANS, CHUNKS, 512, 2 * LANES), BF16),
            pltpu.VMEM((PART, 2 * LANES, LANES), BF16),
            pltpu.VMEM((PART, 512, LANES), F32),
            pltpu.VMEM((PART, LANES, LANES), BF16),
            pltpu.VMEM((GROUPS, DEVICES, PART, LANES), BF16),
            pltpu.SemaphoreType.DMA((5,)),
            pltpu.SemaphoreType.DMA((GROUPS,)),
            pltpu.SemaphoreType.DMA((GROUPS, CHUNKS)),
            pltpu.SemaphoreType.DMA,
            pltpu.SemaphoreType.DMA((GROUPS,)),
            pltpu.SemaphoreType.REGULAR,
            pltpu.SemaphoreType.REGULAR,
            pltpu.SemaphoreType.DMA((GROUPS,)),
            pltpu.SemaphoreType.DMA,
        ],
        compiler_params=pltpu.CompilerParams(collective_id=0, has_side_effects=True, vmem_limit_bytes=56 * 2**20),
        name="beamform",
    )(voltages.reshape(4, DEVICES * GROUPS, PART, LANES), station_map, delay, screen, beam_patch, jnp.asarray(table))
    return pl.pallas_call(
        transpose,
        out_shape=jax.ShapeDtypeStruct((4, 32, DEVICES * CHANS), BF16),
        in_specs=[pl.BlockSpec(memory_space=pltpu.VMEM)],
        out_specs=anywhere,
        scratch_shapes=[
            pltpu.VMEM((STEPS, 4, 32, DEVICES * CHANS // STEPS), BF16),
            pltpu.SemaphoreType.DMA((STEPS,)),
        ],
        name="transpose",
    )(pltpu.with_memory_space_constraint(power, pltpu.VMEM))


def solution(mesh):
    placed = (P(("chan", "beam"), None, None), P(), P(), P(), P())
    return jax.shard_map(
        body, mesh=mesh, in_specs=placed, out_specs=P(("beam", "chan"), None, None), check_vma=False
    )
```

```python
import math

import jax
import jax.numpy as jnp
import numpy as np
from jax import lax
from jax.experimental import pallas as pl
from jax.experimental.pallas import tpu as pltpu
from jax.sharding import PartitionSpec as P

F32, BF16 = jnp.float32, jnp.bfloat16
LOGICAL = pl.DeviceIdType.LOGICAL
STEP = 300.0 / 2048
DEVICES = 128
CHANS = 16
LANES = 128
CHUNKS = 4
PER_CHUNK = DEVICES // CHUNKS
PER_WAIT = PER_CHUNK // 2
GROUPS = 2
UNROLL = 8
STEPS = 4
EMIT_AT = CHUNKS - 1
PART = CHANS // GROUPS
WIDE = 256 // PART


def hops(offset):
    return sum(min(a, 4 - a) for a in offset[:3])


def route():
    lines = [(0, 0, 0)] + [tuple(d * (axis == i) for i in range(3)) for d in (2, 1, 3) for axis in range(3)]
    planes, rest = [], []
    for i in range(9):
        u, v = i % 3 + 1, (i + i // 3) % 3 + 1
        planes += [(u, v, 0), (0, u, v), (v, 0, u)]
    for i in range(27):
        rest.append((i % 3 + 1, (i + i // 3) % 3 + 1, (i + i // 9) % 3 + 1))
    every = [chip + (core,) for chip in lines + planes + rest for core in (1, 0)]
    own = (0, 0, 0, 0)
    return [o for o in every if o != own] + [own]


LINES, PLANES = 19, 54
ROUTE = route()
OUT_ROUTE = sorted(ROUTE, key=lambda o: -hops(o))


def position():
    chan, beam = lax.axis_index("chan"), lax.axis_index("beam")
    return chan // 4, beam % 4, (beam // 4) * 2 + (chan // 2) % 2, chan % 2


def places():
    x, y, z, c = position()
    xs = [(x + d) % 4 for d in range(4)]
    ys = [(y + d) % 4 for d in range(4)]
    zs = [(z + d) % 4 for d in range(4)]
    cs = [(c + d) % 2 for d in range(2)]
    index = ([v * 32 for v in xs], ys, [(v % 2) * 16 + (v // 2) * 4 for v in zs], [v * 8 for v in cs])
    owner = ([v * 4 for v in xs], [v * 16 for v in ys], [(v % 2) * 2 + (v // 2) * 64 for v in zs], cs)
    return index, owner


def at(shares, offset):
    return shares[0][offset[0]] + shares[1][offset[1]] + shares[2][offset[2]] + shares[3][offset[3]]


def fit(fn, odd, terms):
    nodes = (np.cos((2 * np.arange(400) + 1) * np.pi / 800) + 1) / 8
    r = np.sqrt(nodes)
    want = fn(2 * np.pi * r) / (r if odd else 1.0)
    cheb = np.polynomial.chebyshev.Chebyshev.fit(nodes, want, terms - 1, domain=[0, 0.25])
    return [float(v) for v in cheb.convert(kind=np.polynomial.Polynomial).coef]


SIN, COS = fit(np.sin, True, 7), fit(np.cos, False, 8)


def poly(coefs, z):
    total = jnp.full_like(z, coefs[-1])
    for value in coefs[-2::-1]:
        total = total * z + value
    return total


def turn(t):
    r = t - jnp.round(t)
    z = r * r
    return poly(COS, z), r * poly(SIN, z)


def split3(v):
    high = v.astype(BF16)
    rest = v - high.astype(F32)
    mid = rest.astype(BF16)
    low = (rest - mid.astype(F32)).astype(BF16)
    return high, mid, low


def pick(parts, hot, dims):
    total = None
    for part in parts:
        args = (hot, part) if dims == "left" else (part, hot)
        contract = (((0,), (0,)), ((), ())) if dims == "left" else (((1,), (0,)), ((), ()))
        term = lax.dot_general(*args, contract, preferred_element_type=F32)
        total = term if total is None else total + term
    return total


def kernel(
    volt, station_map, delay, screen, beam_patch, offsets, back,
    got, mine_in, delay_in, screen_in, map_in, patch_in, offs_in, delay_at, screen_at, bend, weights, vperm, acc, power,
    sent, load_sem, volt_send, volt_recv, own_sem, lines_in, planes_in, out_send, out_recv,
):
    index, owner = places()
    me = at(index, (0, 0, 0, 0))
    x, y, z, c = position()

    loads = [
        pltpu.make_async_copy(src, dst, load_sem.at[i])
        for i, (src, dst) in enumerate(
            [(station_map, map_in), (offsets, offs_in), (delay, delay_in), (screen, screen_in), (beam_patch, patch_in)]
        )
    ]
    for load in loads:
        load.start()
    barrier = pltpu.get_barrier_semaphore()
    for offset in ROUTE[:LINES]:
        pl.semaphore_signal(barrier, inc=1, device_id=at(index, offset), device_id_type=LOGICAL)
    own = pltpu.make_async_copy(volt.at[:, pl.ds(me * GROUPS, GROUPS), :, :], mine_in, own_sem)
    own.start()
    pl.semaphore_wait(barrier, LINES)

    def send(group, first, last):
        for k, offset in enumerate(ROUTE):
            if not first <= k < last:
                continue
            to = at(index, offset)
            pltpu.make_async_remote_copy(
                src_ref=volt.at[:, to * GROUPS + group, :, :],
                dst_ref=got.at[group, k],
                send_sem=volt_send.at[group],
                recv_sem=volt_recv.at[group, k // PER_WAIT],
                device_id=to,
                device_id_type=LOGICAL,
            ).start()

    for d in (2, 1, 3):
        for offset in ((d, 0, 0, 0), (0, d, 0, 0)):
            pl.semaphore_signal(lines_in, inc=1, device_id=at(index, offset), device_id_type=LOGICAL)
    send(0, 0, LINES)
    pl.semaphore_wait(lines_in, 6)
    for d in (2, 1, 3):
        pl.semaphore_signal(planes_in, inc=1, device_id=at(index, (d, 0, 0, 0)), device_id_type=LOGICAL)
    send(0, LINES, LINES + PLANES)
    for load in loads:
        load.wait()

    col = lax.broadcasted_iota(jnp.int32, (1, 512), 1)
    sx = jnp.bitwise_and(x - offs_in[0:1, :], 3)
    sy = jnp.bitwise_and(y - offs_in[1:2, :], 3)
    sz = jnp.bitwise_and(z - offs_in[2:3, :], 3)
    sc = jnp.bitwise_and(c - offs_in[3:4, :], 1)
    slot = (sx * 32 + sy + jnp.bitwise_and(sz, 1) * 16 + jnp.right_shift(sz, 1) * 4 + sc * 8) * 4
    slot = slot + jnp.bitwise_and(col, 3)
    rows = lax.broadcasted_iota(jnp.int32, (512, 512), 0)
    order = (rows == slot).astype(F32).astype(BF16)
    names = map_in[...].reshape(1, 512)
    tops = jnp.right_shift(names, 4).astype(F32).astype(BF16)
    lows = jnp.bitwise_and(names, 15).astype(F32).astype(BF16)
    halves = jnp.dot(
        jnp.concatenate([jnp.broadcast_to(tops, (16, 512)), jnp.broadcast_to(lows, (16, 512))], axis=0),
        order,
        preferred_element_type=F32,
    )
    station = (halves[0:1] * 16.0 + halves[16:17]).astype(jnp.int32)
    hot = (rows == station).astype(F32).astype(BF16)
    ordered = pick(split3(delay_in[...]), hot, "right")
    for chunk in range(CHUNKS):
        delay_at[chunk] = ordered[:, chunk * LANES : (chunk + 1) * LANES]
    patches = (
        lax.broadcasted_iota(jnp.int32, (64, 512), 0) == patch_in[...].reshape(1, 512)
    ).astype(F32).astype(BF16)
    ordered = pick(split3(pick(split3(screen_in[...]), hot, "right")), patches, "left")
    for chunk in range(CHUNKS):
        screen_at[chunk] = ordered[:, chunk * LANES : (chunk + 1) * LANES]

    pl.semaphore_wait(planes_in, 3)
    send(0, LINES + PLANES, DEVICES - 1)
    send(1, 0, DEVICES - 1)

    first = (lax.broadcasted_iota(jnp.int32, (8, LANES), 0) * 0 + me * CHANS).astype(F32)

    def freq(k):
        return 50.0 + (first + (k + 0.5)) * STEP

    for k in range(CHANS - 2):
        bend[k] = (2.0 * 150.0 * STEP * STEP) / (freq(k) * freq(k + 1) * freq(k + 2))
    tau = 2.0 * math.pi
    scale = 1.0 / math.sqrt(512.0)
    high = 32

    def fill(i, _):
        chunk = i // 16
        block = i % 16
        j = block // 4
        start = j + 4 * high * (block % 4)
        d = delay_at[chunk, pl.ds(start, high, stride=4), :]
        s = screen_at[chunk, pl.ds(start, high, stride=4), :]
        f0, f1 = freq(0)[0:1], freq(1)[0:1]
        c0, s0 = turn(f0 * d + s * ((150.0 / tau) / f0))
        rc, rs = turn(STEP * d - s * ((150.0 / tau) * STEP / (f0 * f1)))
        wr, wi = c0 * scale, s0 * scale
        here = pl.ds(pl.multiple_of(block * high, high), high)
        for k in range(CHANS):
            weights[k, chunk, here, 0:LANES] = wr.astype(BF16)
            weights[k, chunk, here, LANES : 2 * LANES] = wi.astype(BF16)
            if k < CHANS - 1:
                wr, wi = wr * rc - wi * rs, wr * rs + wi * rc
            if k < CHANS - 2:
                turned = s * bend[k, 0:1, :]
                rc, rs = rc - turned * rs, rs + turned * rc
        return 0

    lax.fori_loop(0, 16 * CHUNKS, fill, 0)

    r = lax.broadcasted_iota(jnp.int32, (256, 256), 0)
    q = lax.broadcasted_iota(jnp.int32, (256, 256), 1)
    apart = (r == (q % PART) * WIDE + q // PART).astype(F32).astype(BF16)
    together = (q == (r % PART) * WIDE + r // PART).astype(F32).astype(BF16)
    lane = lax.broadcasted_iota(jnp.int32, (1, LANES), 1)
    low_half = lane < 64
    even = jnp.bitwise_and(lane, 32) == 0
    own.wait()

    def emit(group):
        for offset in OUT_ROUTE[:-1]:
            pltpu.make_async_remote_copy(
                src_ref=sent.at[group, at(owner, offset)],
                dst_ref=back.at[me, group],
                send_sem=out_send.at[group],
                recv_sem=out_recv,
                device_id=at(index, offset),
                device_id_type=LOGICAL,
            ).start()
        keep = pltpu.make_async_copy(sent.at[group, at(owner, (0, 0, 0, 0))], back.at[me, group], own_sem)
        keep.start()
        keep.wait()

    for group in range(GROUPS):
        got[group, DEVICES - 1] = mine_in[:, group]
        for chunk in range(CHUNKS):
            if group and chunk == EMIT_AT:
                emit(group - 1)
            srcs = WIDE // 4
            for m in range(PER_CHUNK // srcs):
                first = chunk * PER_CHUNK + srcs * m
                if first % PER_WAIT == 0:
                    landed = got.at[group, pl.ds(first, min(PER_WAIT, DEVICES - 1 - first))]
                    pltpu.make_async_copy(landed, landed, volt_recv.at[group, first // PER_WAIT]).wait()
                block = got[group, pl.ds(chunk * PER_CHUNK + srcs * m, srcs)].reshape(256, LANES)
                turned = jnp.dot(apart, block, preferred_element_type=F32)
                other = pltpu.roll(turned, 64, 1)
                other = jnp.where(low_half, other, -other)
                here = WIDE * m
                vperm[:, here : here + WIDE, :] = turned.astype(BF16).reshape(PART, WIDE, LANES)
                vperm[:, LANES + here : LANES + here + WIDE, :] = other.astype(BF16).reshape(PART, WIDE, LANES)

            def beams(step, _):
                for u in range(UNROLL):
                    k = step * UNROLL + u
                    part = jnp.dot(weights[group * PART + k, chunk], vperm[k], preferred_element_type=F32)
                    if chunk == 0:
                        acc[k] = part
                    elif chunk < CHUNKS - 1:
                        acc[k] += part
                    else:
                        total = acc[k] + part
                        sq = (total * total).reshape(4, LANES, LANES)
                        one = jnp.where(low_half, sq[0], sq[2])
                        one += pltpu.roll(jnp.where(low_half, sq[2], sq[0]), 64, 1)
                        two = jnp.where(low_half, sq[1], sq[3])
                        two += pltpu.roll(jnp.where(low_half, sq[3], sq[1]), 64, 1)
                        both = jnp.where(even, one, two)
                        both += jnp.where(even, pltpu.roll(one, 96, 1), pltpu.roll(two, 32, 1))
                        power[k] = (0.25 * both).astype(BF16)
                return 0

            lax.fori_loop(0, PART // UNROLL, beams, 0)

        for m in range(DEVICES // WIDE):
            block = power[:, WIDE * m : WIDE * m + WIDE, :].reshape(256, LANES)
            sent[group, WIDE * m : WIDE * m + WIDE] = (
                jnp.dot(together, block, preferred_element_type=F32).astype(BF16).reshape(WIDE, PART, LANES)
            )
        if group == GROUPS - 1:
            emit(group)

    rest = back.at[pl.ds(0, DEVICES - 1)]
    pltpu.make_async_copy(rest, rest, out_recv).wait()
    for group in range(GROUPS):
        gone = got.at[group, pl.ds(0, DEVICES - 1)]
        pltpu.make_async_copy(gone, gone, volt_send.at[group]).wait()
        gone = sent.at[group, pl.ds(0, DEVICES - 1)]
        pltpu.make_async_copy(gone, gone, out_send.at[group]).wait()


def transpose(rows, out, turned, sems):
    eye = (
        lax.broadcasted_iota(jnp.int32, (LANES, LANES), 0) == lax.broadcasted_iota(jnp.int32, (LANES, LANES), 1)
    ).astype(F32).astype(BF16)
    count = DEVICES * CHANS // STEPS
    copies = []
    for i in range(STEPS):
        block = rows[pl.ds(i * DEVICES // STEPS, DEVICES // STEPS)].reshape(count, LANES)
        final = lax.dot_general(eye, block, (((1,), (1,)), ((), ())), preferred_element_type=F32)
        turned[i] = final.astype(BF16).reshape(4, 32, count)
        copy = pltpu.make_async_copy(turned.at[i], out.at[:, :, pl.ds(i * count, count)], sems.at[i])
        copy.start()
        copies.append(copy)
    for copy in copies:
        copy.wait()


def body(voltages, station_map, delay, screen, beam_patch):
    table = np.zeros((8, 512), np.int32)
    for k, offset in enumerate(ROUTE):
        table[:4, 4 * k : 4 * k + 4] = np.array(offset, np.int32)[:, None]
    anywhere = pl.BlockSpec(memory_space=pl.ANY)
    power = pl.pallas_call(
        kernel,
        out_shape=pltpu.VMEM((DEVICES, GROUPS, PART, LANES), BF16),
        in_specs=[anywhere] * 6,
        out_specs=anywhere,
        scratch_shapes=[
            pltpu.VMEM((GROUPS, DEVICES, 4, PART, LANES), BF16),
            pltpu.VMEM((4, GROUPS, PART, LANES), BF16),
            pltpu.VMEM((512, 512), F32),
            pltpu.VMEM((64, 512), F32),
            pltpu.VMEM((512,), jnp.int32),
            pltpu.VMEM((512,), jnp.int32),
            pltpu.VMEM((8, 512), jnp.int32),
            pltpu.VMEM((CHUNKS, 512, LANES), F32),
            pltpu.VMEM((CHUNKS, 512, LANES), F32),
            pltpu.VMEM((CHANS, 8, LANES), F32),
            pltpu.VMEM((CHANS, CHUNKS, 512, 2 * LANES), BF16),
            pltpu.VMEM((PART, 2 * LANES, LANES), BF16),
            pltpu.VMEM((PART, 512, LANES), F32),
            pltpu.VMEM((PART, LANES, LANES), BF16),
            pltpu.VMEM((GROUPS, DEVICES, PART, LANES), BF16),
            pltpu.SemaphoreType.DMA((5,)),
            pltpu.SemaphoreType.DMA((GROUPS,)),
            pltpu.SemaphoreType.DMA((GROUPS, DEVICES // PER_WAIT)),
            pltpu.SemaphoreType.DMA,
            pltpu.SemaphoreType.REGULAR,
            pltpu.SemaphoreType.REGULAR,
            pltpu.SemaphoreType.DMA((GROUPS,)),
            pltpu.SemaphoreType.DMA,
        ],
        compiler_params=pltpu.CompilerParams(collective_id=0, has_side_effects=True, vmem_limit_bytes=56 * 2**20),
        name="beamform",
    )(voltages.reshape(4, DEVICES * GROUPS, PART, LANES), station_map, delay, screen, beam_patch, jnp.asarray(table))
    return pl.pallas_call(
        transpose,
        out_shape=jax.ShapeDtypeStruct((4, 32, DEVICES * CHANS), BF16),
        in_specs=[pl.BlockSpec(memory_space=pltpu.VMEM)],
        out_specs=anywhere,
        scratch_shapes=[
            pltpu.VMEM((STEPS, 4, 32, DEVICES * CHANS // STEPS), BF16),
            pltpu.SemaphoreType.DMA((STEPS,)),
        ],
        name="transpose",
    )(pltpu.with_memory_space_constraint(power, pltpu.VMEM))


def solution(mesh):
    placed = (P(("chan", "beam"), None, None), P(), P(), P(), P())
    return jax.shard_map(
        body, mesh=mesh, in_specs=placed, out_specs=P(("beam", "chan"), None, None), check_vma=False
    )
```
